256 devices in a mesh: dp: 16 (over x_hi, y, core), tensor: 16 (over z, x_lo).
Axes of the slice: x: 4 (x_hi: 2, x_lo: 2; x = x_hi * 2 + x_lo), y: 4, z: 8, core: 2. Of those that a mesh axis runs over, the one named last changes fastest.
Arguments:
- tokens: bfloat16 [16384, 2560], P(('dp', 'tensor')), may hold values from -6 to 6
- gain: float32 [2560], replicated, may hold values from 0.1 to 1.9
- w_qkv: bfloat16 [3, 2560, 2560], P(None, 'tensor'), may hold values from -3 to 3
- w_out: bfloat16 [2560, 2560], P('tensor'), may hold values from -0.125 to 0.125
- cotangent: bfloat16 [16384, 2560], P(('dp', 'tensor')), may hold values from -6 to 6
Outputs:
- output: bfloat16 [16384, 2560], P(('dp', 'tensor'))
- input_gradient: bfloat16 [16384, 2560], P(('dp', 'tensor'))
- grad_qkv: float32 [3, 2560, 2560], P(None, 'tensor')
- grad_out: float32 [2560, 2560], P('tensor')
The draws below stay inside these ranges and needn't reach their ends.
All inputs are finite; a program needn't handle non-finite values.
Results may differ from the reference program's by a relative error of at most 0.023.
Values may be sent and summed in bfloat16 or wider, within the bound.
A program may use at most 128 MiB of HBM per device.

```python
import jax
import jax.numpy as jnp
from jax import lax

D = 2560
HEADS = 32
HEAD_DIM = 80
LEN = 512
MB = 2
TOKENS = 16384
N_DP = 16
N_TENSOR = 16


def draw_w_qkv(key, part):
    key = jax.random.fold_in(key, 7)
    base_key = jax.random.fold_in(key, 0)
    width = HEADS * HEAD_DIM
    weights = jax.random.normal(base_key, (3, width, D), jnp.float32) * D ** (-0.5)
    return weights.astype(jnp.bfloat16)


def block_levels(stream_key, dims, shards, least, largest):
    loudness, own = 1.0, jax.random.fold_in(stream_key, 6)
    for dim, blocks in shards:
        steps = jnp.exp(jax.random.uniform(jax.random.fold_in(own, dim), (blocks,), jnp.float32, least / len(shards), largest / len(shards)))
        loudness = loudness * jnp.repeat(steps, dims[dim] // blocks).reshape([-1 if axis == dim else 1 for axis in range(len(dims))])
    return loudness


def bell_draw(stream_key, extent, deviation, limit, shards=(), kind=jnp.bfloat16):
    drawn = jax.random.normal(stream_key, extent, jnp.float32) * deviation
    if len(shards) > 0:
        drawn = block_levels(stream_key, extent, shards, -0.22, 0.18) * drawn
    return jnp.clip(drawn, min=-limit, max=limit).astype(kind)


def setup_inputs(seed: int = 0) -> dict:
    key_list = jax.random.split(jax.random.key(seed), 6)
    return {
        "tokens": bell_draw(key_list[0], (TOKENS, D), 1.0, 6.0, ((0, 256),)),
        "gain": jnp.clip(1.0 + 0.18 * jax.random.normal(key_list[1], (D,), jnp.float32), 0.1, 1.9),
        "w_qkv": draw_w_qkv(jax.random.fold_in(key_list[5], 71), 0),
        "w_out": bell_draw(key_list[3], (HEADS * HEAD_DIM, D), (HEADS * HEAD_DIM) ** -0.5, 0.125, ((0, 16),)),
        "cotangent": bell_draw(key_list[4], (TOKENS, D), 1.0, 6.0, ((0, 256),)),
    }


def normalize_rows(x, gain):
    xf = x.astype(jnp.float32)
    row_average = lax.optimization_barrier(jnp.mean(xf, axis=-1, keepdims=True))
    centered_rows = xf - row_average
    var = lax.optimization_barrier(jnp.mean(centered_rows * centered_rows, axis=-1, keepdims=True))
    inverse_deviation = lax.rsqrt(var + 1e-05)
    standardized_input = centered_rows * inverse_deviation
    return ((standardized_input * gain).astype(jnp.bfloat16), standardized_input, inverse_deviation)

def split_heads(qkv, heads):
    shaped = qkv.reshape(-1, LEN, 3, heads, HEAD_DIM)
    return (shaped[:, :, 0], shaped[:, :, 1], shaped[:, :, 2])

def attend(query, key, value):
    scale = HEAD_DIM ** (-0.5)
    scores = jnp.einsum('sqhd,skhd->shqk', query.astype(jnp.float32), key.astype(jnp.float32)) * scale
    rows = lax.broadcasted_iota(jnp.int32, (LEN, LEN), 0)
    cols = lax.broadcasted_iota(jnp.int32, (LEN, LEN), 1)
    scores = jnp.where(rows >= cols, scores, -1e+30)
    top = lax.optimization_barrier(jnp.max(scores, axis=-1, keepdims=True))
    expo = jnp.exp(scores - top)
    probs = expo / lax.optimization_barrier(jnp.sum(expo, axis=-1, keepdims=True))
    probs_low = probs.astype(jnp.bfloat16)
    attended = jnp.einsum('shqk,skhd->sqhd', probs_low.astype(jnp.float32), value.astype(jnp.float32)).astype(jnp.bfloat16)
    return (attended, probs, probs_low)

def attend_back(query, key, value, probs, probs_low, d_att):
    scale = HEAD_DIM ** (-0.5)
    d_value = jnp.einsum('shqk,sqhd->skhd', probs_low.astype(jnp.float32), d_att.astype(jnp.float32))
    d_probs = jnp.einsum('sqhd,skhd->shqk', d_att.astype(jnp.float32), value.astype(jnp.float32))
    d_score = probs * (d_probs - lax.optimization_barrier(jnp.sum(d_probs * probs, axis=-1, keepdims=True))) * scale
    d_low = d_score.astype(jnp.bfloat16).astype(jnp.float32)
    d_query = jnp.einsum('shqk,skhd->sqhd', d_low, key.astype(jnp.float32))
    d_key = jnp.einsum('shqk,sqhd->skhd', d_low, query.astype(jnp.float32))
    stacked = jnp.stack([d_query, d_key, d_value], axis=2).astype(jnp.bfloat16)
    return stacked

def reference(tokens, gain, w_qkv, w_out, cotangent):
    width = HEADS * HEAD_DIM
    groups = N_TENSOR
    per_group = width // groups
    rep_rows = MB * LEN
    flat_w = w_qkv.reshape(3 * width, D)

    def replica(pair):
        input_replicated, gradient_replicated = pair
        normalized_rows, standardized_input, inverse_deviation = normalize_rows(input_replicated, gain)
        qkv = jnp.dot(normalized_rows, flat_w.T, preferred_element_type=jnp.float32).astype(jnp.bfloat16)
        query, key, value = split_heads(qkv, HEADS)
        attended, probs, probs_low = attend(query, key, value)
        att_flat = attended.reshape(rep_rows, width)
        parts = jnp.einsum('tgc,gcd->gtd', att_flat.reshape(rep_rows, groups, per_group).astype(jnp.float32), w_out.reshape(groups, per_group, D).astype(jnp.float32)).astype(jnp.bfloat16)
        output = (input_replicated.astype(jnp.float32) + lax.optimization_barrier(jnp.sum(parts.astype(jnp.float32), axis=0))).astype(jnp.bfloat16)
        d_att = jnp.dot(gradient_replicated, w_out.T, preferred_element_type=jnp.float32).astype(jnp.bfloat16)
        grad_out_rep = jnp.dot(att_flat.T, gradient_replicated, preferred_element_type=jnp.float32).astype(jnp.bfloat16)
        d_att = d_att.reshape(MB, LEN, HEADS, HEAD_DIM)
        dqkv = attend_back(query, key, value, probs, probs_low, d_att).reshape(rep_rows, 3 * width)
        grad_qkv_rep = jnp.dot(dqkv.T, normalized_rows, preferred_element_type=jnp.float32).astype(jnp.bfloat16)
        back_parts = jnp.einsum('tjgc,jgcd->gtd', dqkv.reshape(rep_rows, 3, groups, per_group).astype(jnp.float32), w_qkv.reshape(3, groups, per_group, D).astype(jnp.float32)).astype(jnp.bfloat16)
        d_norm = lax.optimization_barrier(jnp.sum(back_parts.astype(jnp.float32), axis=0))
        scaled_rows = d_norm * gain
        first_average = lax.optimization_barrier(jnp.mean(scaled_rows, axis=-1, keepdims=True))
        second_average = lax.optimization_barrier(jnp.mean(scaled_rows * standardized_input, axis=-1, keepdims=True))
        input_gradient = (gradient_replicated.astype(jnp.float32) + inverse_deviation * (scaled_rows - first_average - standardized_input * second_average)).astype(jnp.bfloat16)
        return (output, input_gradient, grad_qkv_rep, grad_out_rep)
    outputs, grads, grad_qkv_reps, grad_out_reps = lax.map(replica, (tokens.reshape(N_DP, rep_rows, D), cotangent.reshape(N_DP, rep_rows, D)))
    grad_qkv = lax.optimization_barrier(jnp.sum(grad_qkv_reps.astype(jnp.float32), axis=0)) / N_DP
    grad_out = lax.optimization_barrier(jnp.sum(grad_out_reps.astype(jnp.float32), axis=0)) / N_DP
    return (outputs.reshape(N_DP * rep_rows, D), grads.reshape(N_DP * rep_rows, D), grad_qkv.reshape(3, width, D), grad_out)
```

```python
import jax
import jax.numpy as jnp
from jax import lax
from jax.experimental import pallas as pl
from jax.experimental.pallas import tpu as pltpu
from jax.sharding import PartitionSpec as P

HEAD_DIM = 80
LEN = 512
MESH = pl.DeviceIdType.MESH
VMEM_BYTES = 56 * 1024 * 1024


def normalize_rows(x, gain):
    xf = x.astype(jnp.float32)
    row_average = jnp.mean(xf, axis=-1, keepdims=True)
    centered_rows = xf - row_average
    var = jnp.mean(centered_rows * centered_rows, axis=-1, keepdims=True)
    inverse_deviation = lax.rsqrt(var + 1e-05)
    standardized_input = centered_rows * inverse_deviation
    return ((standardized_input * gain).astype(jnp.bfloat16), standardized_input, inverse_deviation)


def split_heads(qkv, heads):
    shaped = qkv.reshape(-1, LEN, 3, heads, HEAD_DIM)
    return (shaped[:, :, 0], shaped[:, :, 1], shaped[:, :, 2])


def attend(query, key, value):
    scale = HEAD_DIM ** (-0.5)
    scores = jnp.einsum("sqhd,skhd->shqk", query, key, preferred_element_type=jnp.float32) * scale
    rows = lax.broadcasted_iota(jnp.int32, (LEN, LEN), 0)
    cols = lax.broadcasted_iota(jnp.int32, (LEN, LEN), 1)
    scores = jnp.where(rows >= cols, scores, -1e30)
    top = jnp.max(scores, axis=-1, keepdims=True)
    expo = jnp.exp(scores - top)
    probs = expo / jnp.sum(expo, axis=-1, keepdims=True)
    probs_low = probs.astype(jnp.bfloat16)
    attended = jnp.einsum(
        "shqk,skhd->sqhd", probs_low, value, preferred_element_type=jnp.float32
    ).astype(jnp.bfloat16)
    return (attended, probs, probs_low)


def attend_back(query, key, value, probs, probs_low, d_att):
    scale = HEAD_DIM ** (-0.5)
    d_value = jnp.einsum("shqk,sqhd->skhd", probs_low, d_att, preferred_element_type=jnp.float32)
    d_probs = jnp.einsum("sqhd,skhd->shqk", d_att, value, preferred_element_type=jnp.float32)
    d_score = probs * (d_probs - jnp.sum(d_probs * probs, axis=-1, keepdims=True)) * scale
    d_low = d_score.astype(jnp.bfloat16)
    d_query = jnp.einsum("shqk,skhd->sqhd", d_low, key, preferred_element_type=jnp.float32)
    d_key = jnp.einsum("shqk,sqhd->skhd", d_low, query, preferred_element_type=jnp.float32)
    return jnp.stack([d_query, d_key, d_value], axis=2).astype(jnp.bfloat16)


def inner_rows(left, right):
    return lax.dot_general(
        left, right, (((0,), (0,)), ((), ())), preferred_element_type=jnp.float32
    )


def inner_cols(left, right):
    return lax.dot_general(
        left, right, (((1,), (1,)), ((), ())), preferred_element_type=jnp.float32
    )


class Place:
    def __init__(self):
        dp, tensor = lax.axis_index("dp"), lax.axis_index("tensor")
        self.core = dp % 2
        self.y = (dp // 2) % 4
        self.x_lo = tensor % 2
        self.x = (dp // 8) * 2 + self.x_lo
        self.z = tensor // 2
        self.home = self.core == self.x_lo
        self.away = self.core != self.x_lo

    def at(self, x=None, y=None, z=None, core=None):
        x = self.x if x is None else x
        y = self.y if y is None else y
        z = self.z if z is None else z
        core = self.core if core is None else core
        return ((x // 2) * 8 + y * 2 + core, z * 2 + x % 2)

    def pair(self):
        return self.at(core=1 - self.core)

    def partner(self):
        return self.at(x=self.x + 1 - 2 * self.x_lo, core=1 - self.core)

    def z_next(self, by):
        return self.at(z=(self.z + by + 8) % 8)

    def x_next(self, by):
        return self.at(x=(self.x + by + 4) % 4)

    def y_next(self, by):
        return self.at(y=(self.y + by + 4) % 4)


def greet(devices):
    barrier = pltpu.get_barrier_semaphore()
    for device in devices:
        pl.semaphore_signal(barrier, inc=1, device_id=device, device_id_type=MESH)
    pl.semaphore_wait(barrier, len(devices))


def remote(source, target, send_sem, recv_sem, device):
    return pltpu.make_async_remote_copy(
        src_ref=source,
        dst_ref=target,
        send_sem=send_sem,
        recv_sem=recv_sem,
        device_id=device,
        device_id_type=MESH,
    )


def gather_kernel(
    x_ref,
    c_ref,
    wq_ref,
    wo_ref,
    x_full,
    c_full,
    wq_out,
    wo_out,
    local_sem,
    swap_send,
    swap_recv,
    ring_send,
    ring_recv,
    pair_send,
    pair_recv,
):
    place = Place()
    z, core = place.z, place.core
    rows = x_ref.shape[0]
    half = rows // 2
    up, down = place.z_next(1), place.z_next(-1)
    pair, partner = place.pair(), place.partner()
    greet([up, down, pair, partner])

    def block(full, owner, side, first=0, count=rows):
        owner = (owner + 8) % 8
        start = pl.multiple_of((owner * 2 + side) * rows + first, 32)
        return full.at[pl.ds(start, count), :]

    fulls = (x_full, c_full)
    swapped = [
        (x_ref, block(x_full, z, 1 - core)),
        (c_ref, block(c_full, z, 1 - core)),
        (wq_ref, wq_out),
        (wo_ref, wo_out),
    ]
    kept = [
        (x_ref, block(x_full, z, core)),
        (c_ref, block(c_full, z, core)),
        (wq_ref, wq_out),
        (wo_ref, wo_out),
    ]

    def swap(i):
        return remote(*swapped[i], swap_send.at[i], swap_recv.at[i], partner)

    def keep(i):
        return pltpu.make_async_copy(*kept[i], local_sem.at[i])

    @pl.when(place.away)
    def _():
        for i in range(4):
            swap(i).start()

    @pl.when(place.home)
    def _():
        for i in range(4):
            keep(i).start()

    def settle(i):
        @pl.when(place.away)
        def _():
            swap(i).wait()

        @pl.when(place.home)
        def _():
            keep(i).wait()

    def ring(a, way, k):
        full = fulls[a]
        owner = z - k if way == 0 else z + k
        if k < 3:
            piece = block(full, owner, core)
        else:
            piece = block(full, owner, core, 0 if way == 0 else half, half)
        return remote(
            piece,
            piece,
            ring_send.at[a, way, k],
            ring_recv.at[a, way, k],
            up if way == 0 else down,
        )

    def arrived(a, way, k):
        full = fulls[a]
        owner = z - k - 1 if way == 0 else z + k + 1
        if k < 3:
            return block(full, owner, core)
        return block(full, owner, core, 0 if way == 0 else half, half)

    def to_pair(a, i, piece):
        return remote(piece, piece, pair_send.at[a, i], pair_recv.at[a, i], pair)

    sent = []
    for a in range(2):
        settle(a)
        for way in range(2):
            ring(a, way, 0).start()
        copy = to_pair(a, 0, block(fulls[a], z, core))
        copy.start()
        sent.append(copy)
    for k in range(4):
        for a in range(2):
            for way in range(2):
                ring(a, way, k).wait_recv()
                if k < 3:
                    ring(a, way, k + 1).start()
                copy = to_pair(a, 1 + way * 4 + k, arrived(a, way, k))
                copy.start()
                sent.append(copy)
    settle(2)
    settle(3)
    for a in range(2):
        for way in range(2):
            for k in range(4):
                ring(a, way, k).wait_send()
    for copy in sent:
        copy.wait()


def gather_all(normed, cotangent, flat_w, w_out):
    rows, dim = normed.shape
    any_space = pl.BlockSpec(memory_space=pl.ANY)
    dma = pltpu.SemaphoreType.DMA
    return pl.pallas_call(
        gather_kernel,
        out_shape=(
            jax.ShapeDtypeStruct((rows * 16, dim), jnp.bfloat16),
            jax.ShapeDtypeStruct((rows * 16, dim), jnp.bfloat16),
            jax.ShapeDtypeStruct(flat_w.shape, jnp.bfloat16),
            jax.ShapeDtypeStruct(w_out.shape, jnp.bfloat16),
        ),
        in_specs=[any_space] * 4,
        out_specs=(any_space,) * 4,
        scratch_shapes=[
            dma((4,)),
            dma((4,)),
            dma((4,)),
            dma((2, 2, 4)),
            dma((2, 2, 4)),
            dma((2, 9)),
            dma((2, 9)),
        ],
        compiler_params=pltpu.CompilerParams(collective_id=0, has_side_effects=True),
        name="gather_rows",
    )(normed, cotangent, flat_w, w_out)


def sum_into(target, terms):
    def step(i, carry):
        here = pl.ds(pl.multiple_of(i * 16, 16), 16)
        total = terms[0][here, :].astype(jnp.float32)
        for term in terms[1:]:
            total = total + term[here, :].astype(jnp.float32)
        target[here, :] = total.astype(jnp.bfloat16)
        return carry

    lax.fori_loop(0, target.shape[0] // 16, step, 0)


def reduce_kernel(
    parts_ref,
    back_ref,
    g_ref,
    mixed_out,
    dnorm_out,
    g_out,
    theirs,
    ring_buf,
    final,
    gx_send_buf,
    gx_buf,
    gy_src,
    gy_send_buf,
    gy_buf,
    g_work,
    pair_send,
    pair_recv,
    ring_send,
    ring_recv,
    swap_send,
    swap_recv,
    local_sem,
    gx_send,
    gx_recv,
    gy_send,
    gy_recv,
    ga_send,
    ga_recv,
    gh_send,
    gh_recv,
    gp_send,
    gp_recv,
    g_local,
):
    place = Place()
    x, y, z, core = place.x, place.y, place.z, place.core
    rows = mixed_out.shape[0]
    dim = mixed_out.shape[1]
    half = dim // 2
    up, down = place.z_next(1), place.z_next(-1)
    pair, partner = place.pair(), place.partner()
    right, left, across = place.x_next(1), place.x_next(-1), place.x_next(2)
    north, south = place.y_next(1), place.y_next(-1)
    greet([up, down, pair, partner, right, left, across, north, south])

    sources = (parts_ref, back_ref)
    outs = (mixed_out, dnorm_out)
    wide = (slice(0, half), slice(half, dim))
    all_columns = slice(0, dim)

    def rows_of(owner, side):
        owner = (owner + 8) % 8
        return pl.ds(pl.multiple_of((owner * 2 + side) * rows, 64), rows)

    g_rows = g_ref.shape[0] // 4
    g_cols = dim // 4
    g_half = g_rows // 2
    top, bottom = slice(0, g_half), slice(g_half, g_rows)

    def quarter(q):
        return pl.ds(pl.multiple_of(((q + 4) % 4) * g_rows, 32), g_rows)

    def columns(q):
        return pl.ds(pl.multiple_of(((q + 4) % 4) * g_cols, 128), g_cols)

    def gx(way, k):
        device = right if way == 0 else left
        if k == 0:
            return remote(
                g_ref.at[quarter(x + 2), wide[way]],
                gx_buf.at[way, 0, :, wide[way]],
                gx_send.at[way, 0],
                gx_recv.at[way, 0],
                device,
            )
        return remote(
            gx_send_buf.at[way],
            gx_buf.at[way, 1],
            gx_send.at[way, 1],
            gx_recv.at[way, 1],
            device,
        )

    def gy(way, k):
        device = north if way == 0 else south
        part = top if way == 0 else bottom
        if k == 0:
            return remote(
                gy_src.at[part, columns(y + 2)],
                gy_buf.at[way, 0, part, :],
                gy_send.at[way, 0],
                gy_recv.at[way, 0],
                device,
            )
        return remote(
            gy_send_buf.at[way],
            gy_buf.at[way, 1],
            gy_send.at[way, 1],
            gy_recv.at[way, 1],
            device,
        )

    def ga(way, k):
        device = north if way == 0 else south
        if k == 0:
            spot = g_work.at[quarter(x), columns(y)]
        else:
            first = 0 if way == 0 else g_half
            start = pl.multiple_of(x * g_rows + first, 16)
            spot = g_work.at[pl.ds(start, g_half), columns(y - 1 if way == 0 else y + 1)]
        return remote(spot, spot, ga_send.at[way, k], ga_recv.at[way, k], device)

    def core_copy(a, j):
        owner = z + j
        return remote(
            sources[a].at[rows_of(owner, 1 - core), :],
            theirs.at[a, (owner + 8) % 8],
            pair_send.at[a, j + 3],
            pair_recv.at[a, j + 3],
            pair,
        )

    def ring(a, way, k):
        sign = 1 if way == 0 else -1
        owner = (z + sign * (4 - k) + 8) % 8
        cols = wide[way] if k == 0 else all_columns
        return remote(
            theirs.at[a, owner, :, cols],
            ring_buf.at[a, way, k, :, cols],
            ring_send.at[a, way, k],
            ring_recv.at[a, way, k],
            up if way == 0 else down,
        )

    for way in range(2):
        gx(way, 0).start()
    order = (4, 3, -3, 2, -2, 1, -1, 0)
    for a in range(2):
        for j in order:
            core_copy(a, j).start()

    def sum_step(a, way, k):
        sign = 1 if way == 0 else -1
        j = sign * (4 - k)
        owner = (z + j + 8) % 8
        own, other = sources[a].at[rows_of(owner, core), :], theirs.at[a, owner]
        cols, rest = wide[way], wide[1 - way]
        if k == 0:
            if way == 0:
                core_copy(a, 4).wait_recv()
            sum_into(other.at[:, cols], [own.at[:, cols], other.at[:, cols]])
        else:
            core_copy(a, j).wait_recv()
            ring(a, way, k - 1).wait_recv()
            came = ring_buf.at[a, way, k - 1]
            if k == 1:
                sum_into(other.at[:, cols], [own.at[:, cols], other.at[:, cols], came.at[:, cols]])
                sum_into(other.at[:, rest], [own.at[:, rest], other.at[:, rest]])
            else:
                sum_into(other, [own, other, came])
        ring(a, way, k).start()

    def z_round(k):
        for a in range(2):
            for way in range(2):
                sum_step(a, way, k)

    z_round(0)
    for way in range(2):
        gx(way, 0).wait_recv()
        own = g_ref.at[quarter(x + 1) if way == 0 else quarter(x - 1), :]
        target, came = gx_send_buf.at[way], gx_buf.at[way, 0]
        cols, rest = wide[way], wide[1 - way]
        sum_into(target.at[:, cols], [own.at[:, cols], came.at[:, cols]])
        sum_into(target.at[:, rest], [own.at[:, rest]])
        gx(way, 1).start()
    z_round(1)
    z_round(2)
    for way in range(2):
        gx(way, 1).wait_recv()
    sum_into(gy_src, [g_ref.at[quarter(x), :], gx_buf.at[0, 1], gx_buf.at[1, 1]])
    for way in range(2):
        gy(way, 0).start()
    z_round(3)
    for way in range(2):
        gy(way, 0).wait_recv()
        own = gy_src.at[:, columns(y + 1) if way == 0 else columns(y - 1)]
        target, came = gy_send_buf.at[way], gy_buf.at[way, 0]
        part, rest = (top, bottom) if way == 0 else (bottom, top)
        sum_into(target.at[part, :], [own.at[part, :], came.at[part, :]])
        sum_into(target.at[rest, :], [own.at[rest, :]])
        gy(way, 1).start()
    for way in range(2):
        gy(way, 1).wait_recv()
    spot = g_work.at[quarter(x), columns(y)]
    sum_into(spot, [gy_src.at[:, columns(y)], gy_buf.at[0, 1], gy_buf.at[1, 1]])
    for way in range(2):
        ga(way, 0).start()

    def swap_back(a):
        return remote(final.at[a], outs[a], swap_send.at[a], swap_recv.at[a], partner)

    def keep(a):
        return pltpu.make_async_copy(final.at[a], outs[a], local_sem.at[a])

    for a in range(2):
        core_copy(a, 0).wait_recv()
        ring(a, 0, 3).wait_recv()
        ring(a, 1, 3).wait_recv()
        own = sources[a].at[rows_of(z, core), :]
        sum_into(final.at[a], [own, theirs.at[a, z], ring_buf.at[a, 0, 3], ring_buf.at[a, 1, 3]])

        @pl.when(place.away)
        def _():
            swap_back(a).start()

        @pl.when(place.home)
        def _():
            keep(a).start()

    for way in range(2):
        ga(way, 0).wait_recv()
        ga(way, 1).start()
    for way in range(2):
        ga(way, 1).wait_recv()

    def to_home(i):
        spot = g_work.at[quarter(x), :]
        return remote(spot, spot, gh_send.at[i], gh_recv.at[i], (right, left, across)[i])

    def from_side(i):
        spot = g_work.at[quarter((x - 1, x + 1, x + 2)[i]), :]
        return remote(spot, spot, gh_send.at[i], gh_recv.at[i], pair)

    def handed(i):
        return quarter((x, x - 1, x + 1, x + 2)[i])

    def to_pair(i):
        source, target = g_work.at[handed(i), :], g_out.at[handed(i), :]
        return remote(source, target, gp_send.at[i], gp_recv.at[i], pair)

    def to_out(i):
        return pltpu.make_async_copy(g_work.at[handed(i), :], g_out.at[handed(i), :], g_local.at[i])

    @pl.when(place.away)
    def _():
        to_home(0).start()
        to_home(1).start()
        for a in range(2):
            swap_back(a).wait()
        for i in range(4):
            to_pair(i).wait_recv()
        to_home(0).wait_send()
        to_home(1).wait_send()

    @pl.when(place.home)
    def _():
        to_home(2).start()
        for i in range(4):
            if i > 0:
                from_side(i - 1).wait_recv()
            to_pair(i).start()
            to_out(i).start()
        for a in range(2):
            keep(a).wait()
        for i in range(4):
            to_pair(i).wait_send()
            to_out(i).wait()
        to_home(2).wait_send()

    for a in range(2):
        for j in order:
            core_copy(a, j).wait_send()
        for way in range(2):
            for k in range(4):
                ring(a, way, k).wait_send()
    for way in range(2):
        for k in range(2):
            gx(way, k).wait_send()
            gy(way, k).wait_send()
            ga(way, k).wait_send()


def reduce_all(parts, back_parts, grads):
    dim = parts.shape[1]
    rows = parts.shape[0] // 16
    g_rows, g_cols = grads.shape[0] // 4, dim // 4
    vmem = pl.BlockSpec(memory_space=pltpu.VMEM)
    any_space = pl.BlockSpec(memory_space=pl.ANY)
    dma = pltpu.SemaphoreType.DMA
    low = jnp.bfloat16
    return pl.pallas_call(
        reduce_kernel,
        out_shape=(
            jax.ShapeDtypeStruct((rows, dim), low),
            jax.ShapeDtypeStruct((rows, dim), low),
            jax.ShapeDtypeStruct(grads.shape, low),
        ),
        in_specs=[vmem] * 3,
        out_specs=(any_space,) * 3,
        scratch_shapes=[
            pltpu.VMEM((2, 8, rows, dim), low),
            pltpu.VMEM((2, 2, 4, rows, dim), low),
            pltpu.VMEM((2, rows, dim), low),
            pltpu.VMEM((2, g_rows, dim), low),
            pltpu.VMEM((2, 2, g_rows, dim), low),
            pltpu.VMEM((g_rows, dim), low),
            pltpu.VMEM((2, g_rows, g_cols), low),
            pltpu.VMEM((2, 2, g_rows, g_cols), low),
            pltpu.VMEM(grads.shape, low),
            dma((2, 8)),
            dma((2, 8)),
            dma((2, 2, 4)),
            dma((2, 2, 4)),
            dma((2,)),
            dma((2,)),
            dma((2,)),
            dma((2, 2)),
            dma((2, 2)),
            dma((2, 2)),
            dma((2, 2)),
            dma((2, 2)),
            dma((2, 2)),
            dma((3,)),
            dma((3,)),
            dma((4,)),
            dma((4,)),
            dma((4,)),
        ],
        compiler_params=pltpu.CompilerParams(
            collective_id=1, has_side_effects=True, vmem_limit_bytes=VMEM_BYTES
        ),
        name="reduce_parts",
    )(parts, back_parts, grads)


def per_device(tokens, gain, w_qkv, w_out, cotangent):
    dim = tokens.shape[1]
    width = w_out.shape[0]
    heads = width // HEAD_DIM
    flat_w = w_qkv.reshape(3 * width, dim)
    normalized_rows, standardized_input, inverse_deviation = normalize_rows(tokens, gain)
    normed_full, grad_full, flat_w, w_out = gather_all(normalized_rows, cotangent, flat_w, w_out)
    qkv = inner_cols(normed_full, flat_w).astype(jnp.bfloat16)
    query, key, value = split_heads(qkv, heads)
    attended, probs, probs_low = attend(query, key, value)
    att_flat = attended.reshape(-1, width)
    parts = jnp.dot(att_flat, w_out, preferred_element_type=jnp.float32).astype(jnp.bfloat16)
    d_att = inner_cols(grad_full, w_out).astype(jnp.bfloat16)
    grad_out_part = inner_rows(att_flat, grad_full).astype(jnp.bfloat16)
    d_att = d_att.reshape(-1, LEN, heads, HEAD_DIM)
    dqkv = attend_back(query, key, value, probs, probs_low, d_att).reshape(-1, 3 * width)
    grad_qkv_part = inner_rows(dqkv, normed_full).astype(jnp.bfloat16)
    back_parts = jnp.dot(dqkv, flat_w, preferred_element_type=jnp.float32).astype(jnp.bfloat16)
    grads = jnp.concatenate([grad_qkv_part, grad_out_part], axis=0)
    mixed, d_norm, grad_sums = reduce_all(parts, back_parts, grads)
    output = (tokens.astype(jnp.float32) + mixed.astype(jnp.float32)).astype(jnp.bfloat16)
    replicas = lax.axis_size("dp")
    scaled_rows = d_norm.astype(jnp.float32) * gain
    first_average = jnp.mean(scaled_rows, axis=-1, keepdims=True)
    second_average = jnp.mean(scaled_rows * standardized_input, axis=-1, keepdims=True)
    input_gradient = (
        cotangent.astype(jnp.float32)
        + inverse_deviation * (scaled_rows - first_average - standardized_input * second_average)
    ).astype(jnp.bfloat16)
    grad_sums = grad_sums.astype(jnp.float32) / replicas
    grad_qkv = grad_sums[: 3 * width].reshape(3, width, dim)
    grad_out = grad_sums[3 * width :]
    return (output, input_gradient, grad_qkv, grad_out)


def solution(mesh):
    placed = (
        P(("dp", "tensor"), None),
        P(),
        P(None, "tensor", None),
        P("tensor", None),
        P(("dp", "tensor"), None),
    )
    return jax.shard_map(
        per_device,
        mesh=mesh,
        in_specs=placed,
        out_specs=(
            P(("dp", "tensor"), None),
            P(("dp", "tensor"), None),
            P(None, "tensor", None),
            P("tensor", None),
        ),
        check_vma=False,
    )
```

```python
import jax
import jax.numpy as jnp
from jax import lax
from jax.experimental import pallas as pl
from jax.experimental.pallas import tpu as pltpu
from jax.sharding import PartitionSpec as P

HEAD_DIM = 80
LEN = 512
PAD = 128
BLOCK = 64
SCALE = HEAD_DIM ** (-0.5)
MESH = pl.DeviceIdType.MESH
VMEM_BYTES = 60 * 1024 * 1024
LOW = jnp.bfloat16
WIDE = jnp.float32


class Place:
    def __init__(self):
        dp, tensor = lax.axis_index("dp"), lax.axis_index("tensor")
        self.core = dp % 2
        self.y = (dp // 2) % 4
        self.x_lo = tensor % 2
        self.x = (dp // 8) * 2 + self.x_lo
        self.z = tensor // 2
        self.home = self.core == self.x_lo
        self.away = self.core != self.x_lo

    def at(self, x=None, y=None, z=None, core=None):
        x = self.x if x is None else x
        y = self.y if y is None else y
        z = self.z if z is None else z
        core = self.core if core is None else core
        return ((x // 2) * 8 + y * 2 + core, z * 2 + x % 2)

    def pair(self):
        return self.at(core=1 - self.core)

    def crossed(self, by):
        return self.at(x=(self.x + by + 4) % 4, core=1 - self.core)

    def partner(self):
        return self.crossed(1 - 2 * self.x_lo)

    def z_next(self, by):
        return self.at(z=(self.z + by + 8) % 8)

    def x_next(self, by):
        return self.at(x=(self.x + by + 4) % 4)

    def y_next(self, by):
        return self.at(y=(self.y + by + 4) % 4)


def greet(devices):
    barrier = pltpu.get_barrier_semaphore()
    for device in devices:
        pl.semaphore_signal(barrier, inc=1, device_id=device, device_id_type=MESH)
    pl.semaphore_wait(barrier, len(devices))


def remote(source, target, send_sem, recv_sem, device):
    return pltpu.make_async_remote_copy(
        src_ref=source,
        dst_ref=target,
        send_sem=send_sem,
        recv_sem=recv_sem,
        device_id=device,
        device_id_type=MESH,
    )


def sum_into(target, terms):
    def step(i, carry):
        here = pl.ds(pl.multiple_of(i * 16, 16), 16)
        total = terms[0][here, :].astype(jnp.float32)
        for term in terms[1:]:
            total = total + term[here, :].astype(jnp.float32)
        target[here, :] = total.astype(jnp.bfloat16)
        return carry

    lax.fori_loop(0, target.shape[0] // 16, step, 0)


def nt(left, right):
    return lax.dot_general(left, right, (((1,), (1,)), ((), ())), preferred_element_type=WIDE)


def tn(left, right):
    return lax.dot_general(left, right, (((0,), (0,)), ((), ())), preferred_element_type=WIDE)


def nn(left, right):
    return jnp.dot(left, right, preferred_element_type=WIDE)


def standardize(x):
    xf = x.astype(WIDE)
    centered = xf - jnp.mean(xf, axis=-1, keepdims=True)
    var = jnp.mean(centered * centered, axis=-1, keepdims=True)
    rstd = lax.rsqrt(var + 1e-05)
    return centered * rstd, rstd


def loop(count, body):
    def step(i, carry):
        body(i)
        return carry

    lax.fori_loop(0, count, step, 0)


def layer_kernel(
    tokens,
    gain,
    wq_ref,
    wo_ref,
    cot,
    out_ref,
    ingrad_ref,
    g_out,
    stage,
    x_full,
    c_full,
    wq,
    wo,
    qkv,
    att,
    datt,
    dqkv,
    probs,
    dk_sum,
    dv_sum,
    parts,
    backs,
    theirs,
    first_buf,
    ring_buf,
    final,
    landed,
    g,
    f_first,
    f_buf,
    e_sum,
    s_first,
    s_buf,
    g_work,
    local_sem,
    swap_send,
    swap_recv,
    w_local,
    w_send,
    w_recv,
    gr_send,
    gr_recv,
    gp_send,
    gp_recv,
    core_send,
    core_recv,
    ring_send,
    ring_recv,
    back_send,
    back_recv,
    back_local,
    f_send,
    f_recv,
    s_send,
    s_recv,
    ga_send,
    ga_recv,
    gh_send,
    gh_recv,
    go_send,
    go_recv,
    go_local,
):
    place = Place()
    x, y, z, core = place.x, place.y, place.z, place.core
    dim = tokens.shape[1]
    rows = BLOCK
    half = rows // 2
    mid = dim // 2
    up, down = place.z_next(1), place.z_next(-1)
    pair, partner = place.pair(), place.partner()
    right, left, across = place.x_next(1), place.x_next(-1), place.x_next(2)
    north, south = place.y_next(1), place.y_next(-1)
    cross_right, cross_left = place.crossed(1), place.crossed(-1)

    for i in range(6):
        wq[i * PAD + HEAD_DIM : (i + 1) * PAD, :] = jnp.zeros((PAD - HEAD_DIM, dim), LOW)
    for i in range(2):
        wo[i * PAD + HEAD_DIM : (i + 1) * PAD, :] = jnp.zeros((PAD - HEAD_DIM, dim), LOW)

    def norm_rows(i):
        here = pl.ds(pl.multiple_of(i * 16, 16), 16)
        xhat, _ = standardize(tokens[here, :])
        stage[here, :] = (xhat * gain[...]).astype(LOW)

    loop(rows // 16, norm_rows)
    greet([up, down, pair, cross_right, cross_left, right, left, across, north, south])

    def block(full, owner, side, first=0, count=rows):
        owner = (owner + 8) % 8
        start = pl.multiple_of((owner * 2 + side) * rows + first, 32)
        return full.at[pl.ds(start, count), :]

    fulls, owned = (x_full, c_full), (stage, cot)

    def swap(a):
        target = block(fulls[a], z, 1 - core)
        return remote(owned[a], target, swap_send.at[a], swap_recv.at[a], partner)

    def keep(a):
        return pltpu.make_async_copy(owned[a], block(fulls[a], z, core), local_sem.at[a])

    def weight_ends(i, h):
        if i < 3:
            source = wq_ref.at[i, pl.ds(h * HEAD_DIM, HEAD_DIM), :]
            return source, wq.at[pl.ds((2 * i + h) * PAD, HEAD_DIM), :]
        return wo_ref.at[pl.ds(h * HEAD_DIM, HEAD_DIM), :], wo.at[pl.ds(h * PAD, HEAD_DIM), :]

    def weight_swap(i, h):
        device = cross_right if h == 0 else cross_left
        return remote(*weight_ends(i, h), w_send.at[i, h], w_recv.at[i, h], device)

    def weight_keep(i, h):
        return pltpu.make_async_copy(*weight_ends(i, h), w_local.at[i, h])

    weights = [(i, h) for i in range(4) for h in range(2)]

    @pl.when(place.away)
    def _():
        for a in range(2):
            swap(a).start()
        for i, h in weights:
            weight_swap(i, h).start()

    @pl.when(place.home)
    def _():
        for a in range(2):
            keep(a).start()
        for i, h in weights:
            weight_keep(i, h).start()

    def settle(a):
        @pl.when(place.away)
        def _():
            swap(a).wait_recv()

        @pl.when(place.home)
        def _():
            keep(a).wait()

    def gather_piece(a, way, k, hops):
        owner = z - hops if way == 0 else z + hops
        if k < 3:
            return block(fulls[a], owner, core)
        return block(fulls[a], owner, core, 0 if way == 0 else half, half)

    def gather(a, way, k):
        piece = gather_piece(a, way, k, k)
        device = up if way == 0 else down
        return remote(piece, piece, gr_send.at[a, way, k], gr_recv.at[a, way, k], device)

    def to_pair(a, i):
        if i == 0:
            piece = block(fulls[a], z, core)
        else:
            way, k = (i - 1) // 4, (i - 1) % 4
            piece = gather_piece(a, way, k, k + 1)
        return remote(piece, piece, gp_send.at[a, i], gp_recv.at[a, i], pair)

    def begin(a):
        settle(a)
        for way in range(2):
            gather(a, way, 0).start()
        to_pair(a, 0).start()

    def advance(a, k):
        for way in range(2):
            gather(a, way, k).wait_recv()
            if k < 3:
                gather(a, way, k + 1).start()
            to_pair(a, 1 + way * 4 + k).start()

    def gathered(a):
        for i in range(9):
            to_pair(a, i).wait_recv()

    begin(0)
    for k in range(3):
        advance(0, k)
    begin(1)
    advance(0, 3)

    @pl.when(place.away)
    def _():
        for i, h in weights:
            weight_swap(i, h).wait_recv()

    @pl.when(place.home)
    def _():
        for i, h in weights:
            weight_keep(i, h).wait()

    gathered(0)

    def project(j):
        here = pl.ds(pl.multiple_of(j * 256, 256), 256)
        for i in range(3):
            cols = slice(i * 256, (i + 1) * 256)
            qkv[here, cols] = nt(x_full[here, :], wq[cols, :]).astype(LOW)

    def spots(u):
        r0 = pl.multiple_of((u // 2) * LEN, LEN)
        c0 = pl.multiple_of((u % 2) * PAD, PAD)
        return r0, c0

    def forward(u):
        r0, c0 = spots(u)
        for i in range(4):
            n = (i + 1) * 128
            here = pl.ds(r0 + i * 128, 128)
            query = qkv[here, pl.ds(c0, PAD)]
            key = qkv[pl.ds(r0, n), pl.ds(c0 + 256, PAD)]
            value = qkv[pl.ds(r0, n), pl.ds(c0 + 512, PAD)]
            scores = nt(query, key) * SCALE
            q_at = lax.broadcasted_iota(jnp.int32, (128, n), 0) + i * 128
            k_at = lax.broadcasted_iota(jnp.int32, (128, n), 1)
            scores = jnp.where(q_at >= k_at, scores, -1e30)
            expo = jnp.exp(scores - jnp.max(scores, axis=-1, keepdims=True))
            p = expo * (1.0 / jnp.sum(expo, axis=-1, keepdims=True))
            probs[u, i * 128 : (i + 1) * 128, :n] = p
            att[here, pl.ds(c0, PAD)] = nn(p.astype(LOW), value).astype(LOW)

    def two(first, body):
        loop(2, lambda i: body(first + i))

    two(0, project)
    advance(1, 0)
    two(2, project)
    two(0, forward)
    advance(1, 1)
    two(2, forward)

    def out_parts(j):
        here = pl.ds(pl.multiple_of(j * 256, 256), 256)
        for i in range(10):
            cols = slice(i * 256, (i + 1) * 256)
            parts[here, cols] = nn(att[here, :], wo[:, cols]).astype(LOW)

    loop(4, out_parts)

    sources = (parts, backs)
    wide = (slice(0, mid), slice(mid, dim))
    order = (4, 3, -3, 2, -2, 1, -1, 0)

    def core_copy(a, j):
        owner = (z + j + 8) % 8
        source = block(sources[a], owner, 1 - core)
        return remote(
            source, theirs.at[a, owner], core_send.at[a, j + 3], core_recv.at[a, j + 3], pair
        )

    def ring(a, way, k):
        sign = 1 if way == 0 else -1
        owner = (z + sign * (4 - k) + 8) % 8
        if k == 0:
            source, target = theirs.at[a, owner, :, wide[way]], first_buf.at[a, :, wide[way]]
        else:
            source, target = theirs.at[a, owner], ring_buf.at[a, way, k - 1]
        device = up if way == 0 else down
        return remote(source, target, ring_send.at[a, way, k], ring_recv.at[a, way, k], device)

    def sum_step(a, way, k):
        sign = 1 if way == 0 else -1
        j = sign * (4 - k)
        owner = (z + j + 8) % 8
        own, other = block(sources[a], owner, core), theirs.at[a, owner]
        cols, rest = wide[way], wide[1 - way]
        if k == 0:
            if way == 0:
                core_copy(a, 4).wait_recv()
            sum_into(other.at[:, cols], [own.at[:, cols], other.at[:, cols]])
        else:
            core_copy(a, j).wait_recv()
            ring(a, way, k - 1).wait_recv()
            if k == 1:
                came = first_buf.at[a, :, cols]
                sum_into(other.at[:, cols], [own.at[:, cols], other.at[:, cols], came])
                sum_into(other.at[:, rest], [own.at[:, rest], other.at[:, rest]])
            else:
                sum_into(other, [own, other, ring_buf.at[a, way, k - 2]])
        ring(a, way, k).start()

    def z_round(a, k):
        for way in range(2):
            sum_step(a, way, k)

    def swap_back(a):
        return remote(final.at[a], landed.at[a], back_send.at[a], back_recv.at[a], partner)

    def keep_back(a):
        return pltpu.make_async_copy(final.at[a], landed.at[a], back_local.at[a])

    def z_final(a):
        core_copy(a, 0).wait_recv()
        ring(a, 0, 3).wait_recv()
        ring(a, 1, 3).wait_recv()
        own = block(sources[a], z, core)
        came = [ring_buf.at[a, 0, 2], ring_buf.at[a, 1, 2]]
        sum_into(final.at[a], [own, theirs.at[a, z]] + came)

        @pl.when(place.away)
        def _():
            swap_back(a).start()

        @pl.when(place.home)
        def _():
            keep_back(a).start()

    for j in order:
        core_copy(0, j).start()
    advance(1, 2)
    z_round(0, 0)
    advance(1, 3)
    gathered(1)

    def project_back(j):
        here = pl.ds(pl.multiple_of(j * 256, 256), 256)
        datt[here, :] = nt(c_full[here, :], wo[...]).astype(LOW)

    def backward(u):
        r0, c0 = spots(u)
        for i in (3, 2, 1, 0):
            n = (i + 1) * 128
            here = pl.ds(r0 + i * 128, 128)
            query = qkv[here, pl.ds(c0, PAD)]
            key = qkv[pl.ds(r0, n), pl.ds(c0 + 256, PAD)]
            value = qkv[pl.ds(r0, n), pl.ds(c0 + 512, PAD)]
            d_att = datt[here, pl.ds(c0, PAD)]
            p = probs[u, i * 128 : (i + 1) * 128, :n]
            d_probs = nt(d_att, value)
            d_score = p * (d_probs - jnp.sum(d_probs * p, axis=-1, keepdims=True)) * SCALE
            d_low = d_score.astype(LOW)
            dqkv[here, pl.ds(c0, PAD)] = nn(d_low, key).astype(LOW)
            dk, dv = tn(d_low, query), tn(p.astype(LOW), d_att)
            if i == 3:
                dk_sum[...] = dk
                dv_sum[...] = dv
            else:
                dk_sum[:n, :] += dk
                dv_sum[:n, :] += dv
        dqkv[pl.ds(r0, LEN), pl.ds(c0 + 256, PAD)] = dk_sum[...].astype(LOW)
        dqkv[pl.ds(r0, LEN), pl.ds(c0 + 512, PAD)] = dv_sum[...].astype(LOW)

    loop(4, project_back)
    z_round(0, 1)
    two(0, backward)
    two(2, backward)
    z_round(0, 2)

    for j in range(4):
        lanes = slice(j * 256, (j + 1) * 256)
        for i in range(3):
            backs[i * 256 : (i + 1) * 256, lanes] = dqkv[lanes, i * 256 : (i + 1) * 256].T
        backs[768:1024, lanes] = att[lanes, :].T

    def weight_grads(j):
        cols = pl.ds(pl.multiple_of(j * 256, 256), 256)
        for i in range(4):
            factor = backs[i * 256 : (i + 1) * 256, 0:1024]
            total = nn(factor, (x_full if i < 3 else c_full)[:, cols]).astype(LOW)
            for h in range(2):
                spot = i * 160 + h * HEAD_DIM
                g[spot : spot + HEAD_DIM, cols] = total[h * PAD : h * PAD + HEAD_DIM, :]

    loop(10, weight_grads)

    side_rows, sub, width = 320, 80, dim // 4
    firsts, seconds = (x, y), (y, x)
    neighbours = ((right, left), (north, south))
    top, bottom = slice(0, 160), slice(160, 320)
    sub_top, sub_bottom = slice(0, 48), slice(48, 80)

    def columns(q):
        return pl.ds(pl.multiple_of(((q + 4) % 4) * width, 128), width)

    def g_side(s, q):
        return g.at[pl.ds(s * side_rows, side_rows), columns(q)]

    def sub_rows(q):
        return pl.ds(pl.multiple_of(((q + 4) % 4) * sub, 16), sub)

    def f_copy(s, way, k):
        device = neighbours[s][way]
        sems = (f_send.at[s, way, k], f_recv.at[s, way, k])
        if k == 0:
            part = top if way == 0 else bottom
            return remote(g_side(s, firsts[s] + 2).at[part, :], f_first.at[s, part, :], *sems, device)
        to = firsts[s] + (1 if way == 0 else -1)
        return remote(g_side(s, to), f_buf.at[s, way], *sems, device)

    def s_copy(s, way, k):
        device = neighbours[1 - s][way]
        sems = (s_send.at[s, way, k], s_recv.at[s, way, k])
        if k == 0:
            part = sub_top if way == 0 else sub_bottom
            source = e_sum.at[s, sub_rows(seconds[s] + 2), :].at[part, :]
            return remote(source, s_first.at[s, part, :], *sems, device)
        to = seconds[s] + (1 if way == 0 else -1)
        return remote(e_sum.at[s, sub_rows(to), :], s_buf.at[s, way], *sems, device)

    def f_pass(s):
        for way in range(2):
            f_copy(s, way, 0).wait_recv()
            part = top if way == 0 else bottom
            own = g_side(s, firsts[s] + (1 if way == 0 else -1)).at[part, :]
            sum_into(own, [own, f_first.at[s, part, :]])
            f_copy(s, way, 1).start()

    def f_final(s):
        for way in range(2):
            f_copy(s, way, 1).wait_recv()
        sum_into(e_sum.at[s], [g_side(s, firsts[s]), f_buf.at[s, 0], f_buf.at[s, 1]])
        for way in range(2):
            s_copy(s, way, 0).start()

    def s_pass(s):
        for way in range(2):
            s_copy(s, way, 0).wait_recv()
            part = sub_top if way == 0 else sub_bottom
            to = seconds[s] + (1 if way == 0 else -1)
            own = e_sum.at[s, sub_rows(to), :].at[part, :]
            sum_into(own, [own, s_first.at[s, part, :]])
            s_copy(s, way, 1).start()

    def work(s, row, col, count=sub, first=0):
        start = pl.multiple_of(s * side_rows + ((row + 4) % 4) * sub + first, 16)
        return g_work.at[pl.ds(start, count), columns(col)]

    def work_column(s, col):
        return g_work.at[pl.ds(s * side_rows, side_rows), columns(col)]

    def s_final(s):
        for way in range(2):
            s_copy(s, way, 1).wait_recv()
        own = e_sum.at[s, sub_rows(seconds[s]), :]
        sum_into(work(s, seconds[s], firsts[s]), [own, s_buf.at[s, 0], s_buf.at[s, 1]])

    def ya(s, way, k):
        device = north if way == 0 else south
        if s == 0:
            if k == 0:
                spot = work(0, y, x)
            else:
                count, first = (48, 0) if way == 0 else (32, 48)
                spot = work(0, y - 1 if way == 0 else y + 1, x, count, first)
        else:
            if k == 0:
                spot = work_column(1, y)
            else:
                part = top if way == 0 else bottom
                spot = work_column(1, y - 1 if way == 0 else y + 1).at[part, :]
        return remote(spot, spot, ga_send.at[s, way, k], ga_recv.at[s, way, k], device)

    def xa(s, i):
        spot = work_column(0, x) if s == 0 else work(1, x, y)
        return remote(spot, spot, gh_send.at[s, i], gh_recv.at[s, i], (right, left, across)[i])

    def xa_came(s, i):
        source = (x - 1, x + 1, x + 2)[i]
        spot = work_column(0, source) if s == 0 else work(1, source, y)
        return remote(spot, spot, gh_send.at[s, i], gh_recv.at[s, i], pair)

    def xa_start(s):
        @pl.when(place.away)
        def _():
            xa(s, 0).start()
            xa(s, 1).start()

        @pl.when(place.home)
        def _():
            xa(s, 2).start()

    def handed(s, i):
        at = x if s == 0 else y
        return (pl.ds(s * side_rows, side_rows), columns((at, at - 1, at + 1, at + 2)[i]))

    def hand_pair(s, i):
        spot = handed(s, i)
        return remote(g_work.at[spot], g_out.at[spot], go_send.at[s, i], go_recv.at[s, i], pair)

    def hand_out(s, i):
        spot = handed(s, i)
        return pltpu.make_async_copy(g_work.at[spot], g_out.at[spot], go_local.at[s, i])

    def hand(s, i):
        hand_pair(s, i).start()
        hand_out(s, i).start()

    for s in range(2):
        for way in range(2):
            f_copy(s, way, 0).start()
    z_round(0, 3)

    def back_parts(j):
        here = pl.ds(pl.multiple_of(j * 256, 256), 256)
        for i in range(10):
            cols = slice(i * 256, (i + 1) * 256)
            backs[here, cols] = nn(dqkv[here, :], wq[:, cols]).astype(LOW)

    loop(4, back_parts)
    for j in order:
        core_copy(1, j).start()
    z_round(1, 0)
    for s in range(2):
        f_pass(s)
    z_final(0)
    z_round(1, 1)
    for s in range(2):
        f_final(s)
    z_round(1, 2)
    for s in range(2):
        s_pass(s)
    for s in (1, 0):
        s_final(s)
        if s == 0:
            for way in range(2):
                ya(0, way, 0).start()
        else:
            xa_start(1)
    for way in range(2):
        ya(0, way, 0).wait_recv()
        ya(0, way, 1).start()
    z_round(1, 3)
    for way in range(2):
        ya(0, way, 1).wait_recv()
    xa_start(0)

    @pl.when(place.home)
    def _():
        for i in range(3):
            xa_came(1, i).wait_recv()
        for way in range(2):
            ya(1, way, 0).start()
        hand(1, 0)
        hand(0, 0)
        for way in range(2):
            ya(1, way, 0).wait_recv()
            ya(1, way, 1).start()
            hand(1, 1 + way)

    def landing(a):
        @pl.when(place.away)
        def _():
            swap_back(a).wait_recv()

        @pl.when(place.home)
        def _():
            keep_back(a).wait()

    def finish_output(i):
        here = pl.ds(pl.multiple_of(i * 16, 16), 16)
        out_ref[here, :] = (tokens[here, :].astype(WIDE) + landed[0, here, :].astype(WIDE)).astype(LOW)

    def finish_gradient(i):
        here = pl.ds(pl.multiple_of(i * 16, 16), 16)
        xhat, rstd = standardize(tokens[here, :])
        scaled = landed[1, here, :].astype(WIDE) * gain[...]
        first = jnp.mean(scaled, axis=-1, keepdims=True)
        second = jnp.mean(scaled * xhat, axis=-1, keepdims=True)
        total = cot[here, :].astype(WIDE) + rstd * (scaled - first - xhat * second)
        ingrad_ref[here, :] = total.astype(LOW)

    landing(0)
    loop(rows // 16, finish_output)
    z_final(1)

    @pl.when(place.home)
    def _():
        for way in range(2):
            ya(1, way, 1).wait_recv()
        hand(1, 3)
        for i in range(3):
            xa_came(0, i).wait_recv()
            hand(0, 1 + i)

    landing(1)
    loop(rows // 16, finish_gradient)

    @pl.when(place.away)
    def _():
        for s in range(2):
            for i in range(4):
                hand_pair(s, i).wait_recv()
            xa(s, 0).wait_send()
            xa(s, 1).wait_send()
        for a in range(2):
            swap(a).wait_send()
            swap_back(a).wait_send()
        for i, h in weights:
            weight_swap(i, h).wait_send()

    @pl.when(place.home)
    def _():
        for s in range(2):
            for i in range(4):
                hand_pair(s, i).wait_send()
                hand_out(s, i).wait()
            xa(s, 2).wait_send()
        for way in range(2):
            for k in range(2):
                ya(1, way, k).wait_send()

    for a in range(2):
        for i in range(9):
            to_pair(a, i).wait_send()
        for j in order:
            core_copy(a, j).wait_send()
        for way in range(2):
            for k in range(4):
                gather(a, way, k).wait_send()
                ring(a, way, k).wait_send()
    for way in range(2):
        for k in range(2):
            ya(0, way, k).wait_send()
            for s in range(2):
                f_copy(s, way, k).wait_send()
                s_copy(s, way, k).wait_send()


def run_layer(tokens, gain, w_qkv, w_out, cotangent):
    rows, dim = tokens.shape
    vmem = pl.BlockSpec(memory_space=pltpu.VMEM)
    any_space = pl.BlockSpec(memory_space=pl.ANY)
    dma = pltpu.SemaphoreType.DMA
    sums = 4 * w_out.shape[0]
    quarter = dim // 4

    def low(*shape):
        return pltpu.VMEM(shape, LOW)

    return pl.pallas_call(
        layer_kernel,
        out_shape=(
            jax.ShapeDtypeStruct((rows, dim), LOW),
            jax.ShapeDtypeStruct((rows, dim), LOW),
            jax.ShapeDtypeStruct((sums, dim), LOW),
        ),
        in_specs=[vmem, vmem, any_space, any_space, vmem],
        out_specs=(vmem, vmem, any_space),
        scratch_shapes=[
            low(rows, dim),
            low(rows * 16, dim),
            low(rows * 16, dim),
            low(6 * PAD, dim),
            low(2 * PAD, dim),
            low(rows * 16, 6 * PAD),
            low(rows * 16, 2 * PAD),
            low(rows * 16, 2 * PAD),
            low(rows * 16, 6 * PAD),
            pltpu.VMEM((4, LEN, LEN), WIDE),
            pltpu.VMEM((LEN, PAD), WIDE),
            pltpu.VMEM((LEN, PAD), WIDE),
            low(rows * 16, dim),
            low(rows * 16, dim),
            low(2, 8, rows, dim),
            low(2, rows, dim),
            low(2, 2, 3, rows, dim),
            low(2, rows, dim),
            low(2, rows, dim),
            low(sums, dim),
            low(2, sums // 2, quarter),
            low(2, 2, sums // 2, quarter),
            low(2, sums // 2, quarter),
            low(2, sums // 8, quarter),
            low(2, 2, sums // 8, quarter),
            low(sums, dim),
            dma((2,)),
            dma((2,)),
            dma((2,)),
            dma((4, 2)),
            dma((4, 2)),
            dma((4, 2)),
            dma((2, 2, 4)),
            dma((2, 2, 4)),
            dma((2, 9)),
            dma((2, 9)),
            dma((2, 8)),
            dma((2, 8)),
            dma((2, 2, 4)),
            dma((2, 2, 4)),
            dma((2,)),
            dma((2,)),
            dma((2,)),
            dma((2, 2, 2)),
            dma((2, 2, 2)),
            dma((2, 2, 2)),
            dma((2, 2, 2)),
            dma((2, 2, 2)),
            dma((2, 2, 2)),
            dma((2, 3)),
            dma((2, 3)),
            dma((2, 4)),
            dma((2, 4)),
            dma((2, 4)),
        ],
        compiler_params=pltpu.CompilerParams(
            collective_id=0, has_side_effects=True, vmem_limit_bytes=VMEM_BYTES
        ),
        name="attention_layer",
    )(tokens, gain.reshape(1, dim), w_qkv, w_out, cotangent)


def per_device(tokens, gain, w_qkv, w_out, cotangent):
    width = w_out.shape[0]
    output, input_gradient, sums = run_layer(tokens, gain, w_qkv, w_out, cotangent)
    replicas = lax.axis_size("dp")
    grad_qkv = sums[: 3 * width].astype(jnp.float32) / replicas
    grad_out = sums[3 * width :].astype(jnp.float32) / replicas
    return (output, input_gradient, grad_qkv.reshape(w_qkv.shape), grad_out)


def solution(mesh):
    placed = (
        P(("dp", "tensor"), None),
        P(),
        P(None, "tensor", None),
        P("tensor", None),
        P(("dp", "tensor"), None),
    )
    return jax.shard_map(
        per_device,
        mesh=mesh,
        in_specs=placed,
        out_specs=(
            P(("dp", "tensor"), None),
            P(("dp", "tensor"), None),
            P(None, "tensor", None),
            P("tensor", None),
        ),
        check_vma=False,
    )
```

```python
import jax
import jax.numpy as jnp
from jax import lax
from jax.experimental import pallas as pl
from jax.experimental.pallas import tpu as pltpu
from jax.sharding import PartitionSpec as P

HEAD_DIM = 80
LEN = 512
PAD = 128
BLOCK = 64
SCALE = HEAD_DIM ** (-0.5)
MESH = pl.DeviceIdType.MESH
VMEM_BYTES = 60 * 1024 * 1024
LOW = jnp.bfloat16
WIDE = jnp.float32


class Place:
    def __init__(self):
        dp, tensor = lax.axis_index("dp"), lax.axis_index("tensor")
        self.core = dp % 2
        self.y = (dp // 2) % 4
        self.x_lo = tensor % 2
        self.x = (dp // 8) * 2 + self.x_lo
        self.z = tensor // 2
        self.home = self.core == self.x_lo
        self.away = self.core != self.x_lo

    def at(self, x=None, y=None, z=None, core=None):
        x = self.x if x is None else x
        y = self.y if y is None else y
        z = self.z if z is None else z
        core = self.core if core is None else core
        return ((x // 2) * 8 + y * 2 + core, z * 2 + x % 2)

    def pair(self):
        return self.at(core=1 - self.core)

    def crossed(self, by):
        return self.at(x=(self.x + by + 4) % 4, core=1 - self.core)

    def partner(self):
        return self.crossed(1 - 2 * self.x_lo)

    def z_next(self, by):
        return self.at(z=(self.z + by + 8) % 8)

    def x_next(self, by):
        return self.at(x=(self.x + by + 4) % 4)

    def y_next(self, by):
        return self.at(y=(self.y + by + 4) % 4)


def greet(devices):
    barrier = pltpu.get_barrier_semaphore()
    for device in devices:
        pl.semaphore_signal(barrier, inc=1, device_id=device, device_id_type=MESH)
    pl.semaphore_wait(barrier, len(devices))


def remote(source, target, send_sem, recv_sem, device):
    return pltpu.make_async_remote_copy(
        src_ref=source,
        dst_ref=target,
        send_sem=send_sem,
        recv_sem=recv_sem,
        device_id=device,
        device_id_type=MESH,
    )


def sum_into(target, terms):
    def step(i, carry):
        here = pl.ds(pl.multiple_of(i * 16, 16), 16)
        total = terms[0][here, :].astype(jnp.float32)
        for term in terms[1:]:
            total = total + term[here, :].astype(jnp.float32)
        target[here, :] = total.astype(jnp.bfloat16)
        return carry

    lax.fori_loop(0, target.shape[0] // 16, step, 0)


def nt(left, right):
    return lax.dot_general(left, right, (((1,), (1,)), ((), ())), preferred_element_type=WIDE)


def tn(left, right):
    return lax.dot_general(left, right, (((0,), (0,)), ((), ())), preferred_element_type=WIDE)


def nn(left, right):
    return jnp.dot(left, right, preferred_element_type=WIDE)


def standardize(x):
    xf = x.astype(WIDE)
    centered = xf - jnp.mean(xf, axis=-1, keepdims=True)
    var = jnp.mean(centered * centered, axis=-1, keepdims=True)
    rstd = lax.rsqrt(var + 1e-05)
    return centered * rstd, rstd


def loop(count, body):
    def step(i, carry):
        body(i)
        return carry

    lax.fori_loop(0, count, step, 0)


def layer_kernel(
    tokens,
    gain,
    wq_ref,
    wo_ref,
    cot,
    out_ref,
    ingrad_ref,
    g_out,
    stage,
    x_full,
    c_full,
    wq,
    wo,
    qkv,
    att,
    datt,
    dqkv,
    probs,
    dk_sum,
    dv_sum,
    parts,
    backs,
    theirs,
    first_buf,
    ring_buf,
    final,
    landed,
    g,
    f_first,
    f_buf,
    e_sum,
    s_first,
    s_buf,
    g_work,
    local_sem,
    swap_send,
    swap_recv,
    w_local,
    w_send,
    w_recv,
    gr_send,
    gr_recv,
    go_pair_send,
    go_pair_recv,
    gp_send,
    gp_recv,
    core_send,
    core_recv,
    ring_send,
    ring_recv,
    back_send,
    back_recv,
    back_local,
    f_send,
    f_recv,
    s_send,
    s_recv,
    ga_send,
    ga_recv,
    gh_send,
    gh_recv,
    go_send,
    go_recv,
    go_local,
):
    place = Place()
    x, y, z, core = place.x, place.y, place.z, place.core
    dim = tokens.shape[1]
    rows = BLOCK
    half = rows // 2
    up, down = place.z_next(1), place.z_next(-1)
    pair, partner = place.pair(), place.partner()
    right, left, across = place.x_next(1), place.x_next(-1), place.x_next(2)
    north, south = place.y_next(1), place.y_next(-1)
    cross_right, cross_left = place.crossed(1), place.crossed(-1)

    for i in range(6):
        wq[i * PAD + HEAD_DIM : (i + 1) * PAD, :] = jnp.zeros((PAD - HEAD_DIM, dim), LOW)
    for i in range(2):
        wo[i * PAD + HEAD_DIM : (i + 1) * PAD, :] = jnp.zeros((PAD - HEAD_DIM, dim), LOW)

    def norm_rows(i):
        here = pl.ds(pl.multiple_of(i * 16, 16), 16)
        xhat, _ = standardize(tokens[here, :])
        stage[here, :] = (xhat * gain[...]).astype(LOW)

    loop(rows // 16, norm_rows)
    greet([up, down, pair, cross_right, cross_left, right, left, across, north, south])

    def block(full, owner, side, first=0, count=rows):
        owner = (owner + 8) % 8
        start = pl.multiple_of((owner * 2 + side) * rows + first, 32)
        return full.at[pl.ds(start, count), :]

    chunks = (slice(0, half), slice(half, rows))
    both = ((0, 0), (0, 1), (1, 0), (1, 1))
    fulls, owned = (x_full, c_full), (stage, cot)

    def hops(way, q):
        return 4 if way == q else 3

    def swap(a, q):
        target = block(fulls[a], z, 1 - core, q * half, half)
        source = owned[a].at[chunks[q], :]
        return remote(source, target, swap_send.at[a, q], swap_recv.at[a, q], partner)

    def keep(a, q):
        target = block(fulls[a], z, core, q * half, half)
        return pltpu.make_async_copy(owned[a].at[chunks[q], :], target, local_sem.at[a, q])

    def weight_ends(i, h):
        if i < 3:
            source = wq_ref.at[i, pl.ds(h * HEAD_DIM, HEAD_DIM), :]
            return source, wq.at[pl.ds((2 * i + h) * PAD, HEAD_DIM), :]
        return wo_ref.at[pl.ds(h * HEAD_DIM, HEAD_DIM), :], wo.at[pl.ds(h * PAD, HEAD_DIM), :]

    def weight_swap(i, h):
        device = cross_right if h == 0 else cross_left
        return remote(*weight_ends(i, h), w_send.at[i, h], w_recv.at[i, h], device)

    def weight_keep(i, h):
        return pltpu.make_async_copy(*weight_ends(i, h), w_local.at[i, h])

    weights = [(i, h) for i in range(4) for h in range(2)]

    @pl.when(place.away)
    def _():
        for a, q in both:
            swap(a, q).start()
        for i, h in weights:
            weight_swap(i, h).start()

    @pl.when(place.home)
    def _():
        for a, q in both:
            keep(a, q).start()
        for i, h in weights:
            weight_keep(i, h).start()

    def gather_piece(a, way, hop, q):
        return block(fulls[a], z - hop if way == 0 else z + hop, core, q * half, half)

    def gather(a, way, k, q):
        piece = gather_piece(a, way, k, q)
        device = up if way == 0 else down
        return remote(piece, piece, gr_send.at[a, way, k, q], gr_recv.at[a, way, k, q], device)

    def own_pair(a, q):
        piece = gather_piece(a, 0, 0, q)
        return remote(piece, piece, go_pair_send.at[a, q], go_pair_recv.at[a, q], pair)

    def to_pair(a, way, k, q):
        piece = gather_piece(a, way, k + 1, q)
        return remote(piece, piece, gp_send.at[a, way, k, q], gp_recv.at[a, way, k, q], pair)

    def begin(a, q):
        @pl.when(place.away)
        def _():
            swap(a, q).wait_recv()

        @pl.when(place.home)
        def _():
            keep(a, q).wait()

        for way in range(2):
            gather(a, way, 0, q).start()
        own_pair(a, q).start()

    def advance(a, k, q):
        for way in range(2):
            if k < hops(way, q):
                gather(a, way, k, q).wait_recv()
                if k + 1 < hops(way, q):
                    gather(a, way, k + 1, q).start()
                to_pair(a, way, k, q).start()

    hop_list = [(way, k, q) for k in range(4) for q in range(2) for way in range(2) if k < hops(way, q)]

    def gathered(a):
        for q in range(2):
            own_pair(a, q).wait_recv()
        for way, k, q in hop_list:
            to_pair(a, way, k, q).wait_recv()

    for q in range(2):
        begin(0, q)
    for k in range(3):
        for q in range(2):
            advance(0, k, q)
    for q in range(2):
        begin(1, q)
    for q in range(2):
        advance(0, 3, q)

    @pl.when(place.away)
    def _():
        for i, h in weights:
            weight_swap(i, h).wait_recv()

    @pl.when(place.home)
    def _():
        for i, h in weights:
            weight_keep(i, h).wait()

    gathered(0)

    def project(j):
        here = pl.ds(pl.multiple_of(j * 256, 256), 256)
        for i in range(3):
            cols = slice(i * 256, (i + 1) * 256)
            qkv[here, cols] = nt(x_full[here, :], wq[cols, :]).astype(LOW)

    def spots(u):
        r0 = pl.multiple_of((u // 2) * LEN, LEN)
        c0 = pl.multiple_of((u % 2) * PAD, PAD)
        return r0, c0

    def forward(u):
        r0, c0 = spots(u)
        for i in range(4):
            n = (i + 1) * 128
            here = pl.ds(r0 + i * 128, 128)
            query = qkv[here, pl.ds(c0, PAD)]
            key = qkv[pl.ds(r0, n), pl.ds(c0 + 256, PAD)]
            value = qkv[pl.ds(r0, n), pl.ds(c0 + 512, PAD)]
            scores = nt(query, key) * SCALE
            q_at = lax.broadcasted_iota(jnp.int32, (128, n), 0) + i * 128
            k_at = lax.broadcasted_iota(jnp.int32, (128, n), 1)
            scores = jnp.where(q_at >= k_at, scores, -1e30)
            expo = jnp.exp(scores - jnp.max(scores, axis=-1, keepdims=True))
            p = expo * (1.0 / jnp.sum(expo, axis=-1, keepdims=True))
            probs[u, i * 128 : (i + 1) * 128, :n] = p
            att[here, pl.ds(c0, PAD)] = nn(p.astype(LOW), value).astype(LOW)

    def one(at, body):
        loop(1, lambda i: body(at + i))

    def two(first, body):
        loop(2, lambda i: body(first + i))

    def out_parts(j):
        here = pl.ds(pl.multiple_of(j * 256, 256), 256)
        for i in range(10):
            cols = slice(i * 256, (i + 1) * 256)
            parts[here, cols] = nn(att[here, :], wo[:, cols]).astype(LOW)

    sources = (parts, backs)
    near = ((z + 4) % 8) // 2
    groups = (near, (near + 1) % 4, (near + 3) % 4, (near + 2) % 4)
    order = (4, 3, -3, 2, -2, 1, -1, 0)

    def core_copy(a, j):
        owner = (z + j + 8) % 8
        source = block(sources[a], owner, 1 - core)
        return remote(
            source, theirs.at[a, owner], core_send.at[a, j + 3], core_recv.at[a, j + 3], pair
        )

    def ring(a, way, k, q):
        sign = 1 if way == 0 else -1
        owner = (z + sign * (4 - k) + 8) % 8
        source = theirs.at[a, owner, chunks[q], :]
        if k == 0:
            target = first_buf.at[a, chunks[q], :]
        else:
            target = ring_buf.at[a, way, k - 1, chunks[q], :]
        device = up if way == 0 else down
        return remote(source, target, ring_send.at[a, way, k, q], ring_recv.at[a, way, k, q], device)

    def z_step(a, k, q):
        for way in range(2):
            if k < 4 - hops(way, q):
                continue
            j = (4 - k) * (1 if way == 0 else -1)
            owner = (z + j + 8) % 8
            own = block(sources[a], owner, core, q * half, half)
            other = theirs.at[a, owner, chunks[q], :]
            terms = [own, other]
            if k == 0:
                if q == 0:
                    core_copy(a, 4).wait_recv()
            else:
                if q == 0:
                    core_copy(a, j).wait_recv()
                if k > 4 - hops(way, q):
                    ring(a, way, k - 1, q).wait_recv()
                    if k == 1:
                        terms.append(first_buf.at[a, chunks[q], :])
                    else:
                        terms.append(ring_buf.at[a, way, k - 2, chunks[q], :])
            sum_into(other, terms)
            ring(a, way, k, q).start()

    send_list = [(way, k, q) for k in range(4) for q in range(2) for way in range(2) if k >= 4 - hops(way, q)]

    def swap_back(a, q):
        source, target = final.at[a, chunks[q], :], landed.at[a, chunks[q], :]
        return remote(source, target, back_send.at[a, q], back_recv.at[a, q], partner)

    def keep_back(a, q):
        source, target = final.at[a, chunks[q], :], landed.at[a, chunks[q], :]
        return pltpu.make_async_copy(source, target, back_local.at[a, q])

    def z_final(a, q):
        if q == 0:
            core_copy(a, 0).wait_recv()
        terms = [block(sources[a], z, core, q * half, half), theirs.at[a, z, chunks[q], :]]
        for way in range(2):
            ring(a, way, 3, q).wait_recv()
            terms.append(ring_buf.at[a, way, 2, chunks[q], :])
        sum_into(final.at[a, chunks[q], :], terms)

        @pl.when(place.away)
        def _():
            swap_back(a, q).start()

        @pl.when(place.home)
        def _():
            keep_back(a, q).start()

    def core_copies(a, js):
        for j in js:
            core_copy(a, j).start()

    one(0, project)
    advance(1, 0, 0)
    one(1, project)
    advance(1, 0, 1)
    one(2, project)
    advance(1, 1, 0)
    one(3, project)
    advance(1, 1, 1)
    one(0, forward)
    one(1, forward)
    advance(1, 2, 0)
    one(2, forward)
    one(3, forward)
    advance(1, 2, 1)
    one(groups[0], out_parts)
    core_copies(0, (4,))
    one(groups[1], out_parts)
    one(groups[2], out_parts)
    core_copies(0, (3, -3, 2, -2))
    z_step(0, 0, 0)
    z_step(0, 0, 1)
    one(groups[3], out_parts)
    core_copies(0, (1, -1, 0))
    advance(1, 3, 0)
    advance(1, 3, 1)
    gathered(1)

    def project_back(j):
        here = pl.ds(pl.multiple_of(j * 256, 256), 256)
        datt[here, :] = nt(c_full[here, :], wo[...]).astype(LOW)

    def backward(u):
        r0, c0 = spots(u)
        for i in (3, 2, 1, 0):
            n = (i + 1) * 128
            here = pl.ds(r0 + i * 128, 128)
            query = qkv[here, pl.ds(c0, PAD)]
            key = qkv[pl.ds(r0, n), pl.ds(c0 + 256, PAD)]
            value = qkv[pl.ds(r0, n), pl.ds(c0 + 512, PAD)]
            d_att = datt[here, pl.ds(c0, PAD)]
            p = probs[u, i * 128 : (i + 1) * 128, :n]
            d_probs = nt(d_att, value)
            d_score = p * (d_probs - jnp.sum(d_probs * p, axis=-1, keepdims=True)) * SCALE
            d_low = d_score.astype(LOW)
            dqkv[here, pl.ds(c0, PAD)] = nn(d_low, key).astype(LOW)
            dk, dv = tn(d_low, query), tn(p.astype(LOW), d_att)
            if i == 3:
                dk_sum[...] = dk
                dv_sum[...] = dv
            else:
                dk_sum[:n, :] += dk
                dv_sum[:n, :] += dv
        dqkv[pl.ds(r0, LEN), pl.ds(c0 + 256, PAD)] = dk_sum[...].astype(LOW)
        dqkv[pl.ds(r0, LEN), pl.ds(c0 + 512, PAD)] = dv_sum[...].astype(LOW)

    loop(4, project_back)
    z_step(0, 1, 0)
    one(0, backward)
    z_step(0, 1, 1)
    two(1, backward)
    z_step(0, 2, 0)
    one(3, backward)
    z_step(0, 2, 1)

    for j in range(4):
        lanes = slice(j * 256, (j + 1) * 256)
        for i in range(3):
            backs[i * 256 : (i + 1) * 256, lanes] = dqkv[lanes, i * 256 : (i + 1) * 256].T
        backs[768:1024, lanes] = att[lanes, :].T

    def weight_grads(j):
        cols = pl.ds(pl.multiple_of(j * 256, 256), 256)
        for i in range(4):
            factor = backs[i * 256 : (i + 1) * 256, 0:1024]
            total = nn(factor, (x_full if i < 3 else c_full)[:, cols]).astype(LOW)
            for h in range(2):
                spot = i * 160 + h * HEAD_DIM
                g[spot : spot + HEAD_DIM, cols] = total[h * PAD : h * PAD + HEAD_DIM, :]

    two(0, weight_grads)
    z_step(0, 3, 0)
    loop(8, lambda j: weight_grads(j + 2))

    side_start, side_rows, subs, width = (0, 256), (256, 384), (64, 96), dim // 4
    firsts, seconds = (x, y), (y, x)
    neighbours = ((right, left), (north, south))
    lanes = (slice(0, 384), slice(384, 640))
    pieces = [(s, c) for c in range(2) for s in range(2)]

    def half_of(s, way, size):
        count = size[s] // 2
        return slice(way * count, (way + 1) * count)

    def columns(q):
        return pl.ds(pl.multiple_of(((q + 4) % 4) * width, 128), width)

    def g_side(s, q, c):
        return g.at[pl.ds(side_start[s], side_rows[s]), columns(q)].at[:, lanes[c]]

    def sub_rows(s, q):
        return pl.ds(pl.multiple_of(((q + 4) % 4) * subs[s], 32), subs[s])

    def e_sub(s, q, c):
        return e_sum.at[s, sub_rows(s, q), lanes[c]]

    def step_to(s, way, places):
        return places[s] + (1 if way == 0 else -1)

    def f_copy(s, way, k, c):
        device = neighbours[s][way]
        sems = (f_send.at[s, way, k, c], f_recv.at[s, way, k, c])
        if k == 0:
            part = half_of(s, way, side_rows)
            source = g_side(s, firsts[s] + 2, c).at[part, :]
            return remote(source, f_first.at[s, part, lanes[c]], *sems, device)
        source = g_side(s, step_to(s, way, firsts), c)
        return remote(source, f_buf.at[s, way, 0 : side_rows[s], lanes[c]], *sems, device)

    def s_copy(s, way, k, c):
        device = neighbours[1 - s][way]
        sems = (s_send.at[s, way, k, c], s_recv.at[s, way, k, c])
        if k == 0:
            part = half_of(s, way, subs)
            source = e_sub(s, seconds[s] + 2, c).at[part, :]
            return remote(source, s_first.at[s, part, lanes[c]], *sems, device)
        source = e_sub(s, step_to(s, way, seconds), c)
        return remote(source, s_buf.at[s, way, 0 : subs[s], lanes[c]], *sems, device)

    def f_pass(s, c):
        for way in range(2):
            f_copy(s, way, 0, c).wait_recv()
            part = half_of(s, way, side_rows)
            own = g_side(s, step_to(s, way, firsts), c).at[part, :]
            sum_into(own, [own, f_first.at[s, part, lanes[c]]])
            f_copy(s, way, 1, c).start()

    def f_final(s, c):
        for way in range(2):
            f_copy(s, way, 1, c).wait_recv()
        came = [f_buf.at[s, way, 0 : side_rows[s], lanes[c]] for way in range(2)]
        sum_into(e_sum.at[s, 0 : side_rows[s], lanes[c]], [g_side(s, firsts[s], c)] + came)
        for way in range(2):
            s_copy(s, way, 0, c).start()

    def s_pass(s, c):
        for way in range(2):
            s_copy(s, way, 0, c).wait_recv()
            part = half_of(s, way, subs)
            own = e_sub(s, step_to(s, way, seconds), c).at[part, :]
            sum_into(own, [own, s_first.at[s, part, lanes[c]]])
            s_copy(s, way, 1, c).start()

    def work(s, row, col, c):
        start = pl.multiple_of(side_start[s] + ((row + 4) % 4) * subs[s], 32)
        return g_work.at[pl.ds(start, subs[s]), columns(col)].at[:, lanes[c]]

    def work_column(s, col, c):
        return g_work.at[pl.ds(side_start[s], side_rows[s]), columns(col)].at[:, lanes[c]]

    def s_final(s, c):
        for way in range(2):
            s_copy(s, way, 1, c).wait_recv()
        came = [s_buf.at[s, way, 0 : subs[s], lanes[c]] for way in range(2)]
        sum_into(work(s, seconds[s], firsts[s], c), [e_sub(s, seconds[s], c)] + came)

    def ya(s, way, k, c):
        device = north if way == 0 else south
        at = y if k == 0 else (y - 1 if way == 0 else y + 1)
        if s == 0:
            spot, size = work(0, at, x, c), subs
        else:
            spot, size = work_column(1, at, c), side_rows
        if k == 1:
            spot = spot.at[half_of(s, way, size), :]
        return remote(spot, spot, ga_send.at[s, way, k, c], ga_recv.at[s, way, k, c], device)

    def xa(s, i, c):
        spot = work_column(0, x, c) if s == 0 else work(1, x, y, c)
        device = (right, left, across)[i]
        return remote(spot, spot, gh_send.at[s, i, c], gh_recv.at[s, i, c], device)

    def xa_came(s, i, c):
        source = (x - 1, x + 1, x + 2)[i]
        spot = work_column(0, source, c) if s == 0 else work(1, source, y, c)
        return remote(spot, spot, gh_send.at[s, i, c], gh_recv.at[s, i, c], pair)

    def xa_start(s, c):
        @pl.when(place.away)
        def _():
            xa(s, 0, c).start()
            xa(s, 1, c).start()

        @pl.when(place.home)
        def _():
            xa(s, 2, c).start()

    def handed(s, i, c):
        at = x if s == 0 else y
        place_of = columns((at, at - 1, at + 1, at + 2)[i])
        return lambda ref: ref.at[pl.ds(side_start[s], side_rows[s]), place_of].at[:, lanes[c]]

    def hand_pair(s, i, c):
        spot = handed(s, i, c)
        return remote(spot(g_work), spot(g_out), go_send.at[s, i, c], go_recv.at[s, i, c], pair)

    def hand_out(s, i, c):
        spot = handed(s, i, c)
        return pltpu.make_async_copy(spot(g_work), spot(g_out), go_local.at[s, i, c])

    def hand(s, i, c):
        hand_pair(s, i, c).start()
        hand_out(s, i, c).start()

    def y_start(c):
        for way in range(2):
            ya(0, way, 0, c).start()
        xa_start(1, c)

    def y_pass(c):
        for way in range(2):
            ya(0, way, 0, c).wait_recv()
            ya(0, way, 1, c).start()

    def y_final(c):
        for way in range(2):
            ya(0, way, 1, c).wait_recv()
        xa_start(0, c)

    for s, c in pieces:
        for way in range(2):
            f_copy(s, way, 0, c).start()

    def back_parts(j):
        here = pl.ds(pl.multiple_of(j * 256, 256), 256)
        for i in range(10):
            cols = slice(i * 256, (i + 1) * 256)
            backs[here, cols] = nn(dqkv[here, :], wq[:, cols]).astype(LOW)

    z_step(0, 3, 1)
    one(groups[0], back_parts)
    core_copies(1, (4,))
    f_pass(0, 0)
    f_pass(1, 0)
    one(groups[1], back_parts)
    z_step(1, 0, 0)
    z_step(1, 0, 1)
    one(groups[2], back_parts)
    core_copies(1, (3, -3, 2, -2))
    f_pass(0, 1)
    f_pass(1, 1)
    z_final(0, 0)
    z_step(1, 1, 0)
    one(groups[3], back_parts)
    core_copies(1, (1, -1, 0))
    z_final(0, 1)
    z_step(1, 1, 1)
    f_final(0, 0)
    f_final(1, 0)
    z_step(1, 2, 0)
    s_pass(0, 0)
    s_pass(1, 0)
    f_final(0, 1)
    f_final(1, 1)
    z_step(1, 2, 1)
    s_pass(0, 1)
    s_pass(1, 1)
    s_final(0, 0)
    s_final(1, 0)
    y_start(0)
    z_step(1, 3, 0)
    s_final(0, 1)
    s_final(1, 1)
    y_start(1)
    y_pass(0)
    z_step(1, 3, 1)
    y_pass(1)
    y_final(0)

    @pl.when(place.home)
    def _():
        for c in range(2):
            for i in range(3):
                xa_came(1, i, c).wait_recv()
            for way in range(2):
                ya(1, way, 0, c).start()
            hand(1, 0, c)
            if c == 0:
                hand(0, 0, 0)

    y_final(1)

    @pl.when(place.home)
    def _():
        hand(0, 0, 1)
        for c in range(2):
            for way in range(2):
                ya(1, way, 0, c).wait_recv()
                ya(1, way, 1, c).start()
                hand(1, 1 + way, c)

    def landing(a):
        @pl.when(place.away)
        def _():
            for q in range(2):
                swap_back(a, q).wait_recv()

        @pl.when(place.home)
        def _():
            for q in range(2):
                keep_back(a, q).wait()

    def finish_output(i):
        here = pl.ds(pl.multiple_of(i * 16, 16), 16)
        out_ref[here, :] = (tokens[here, :].astype(WIDE) + landed[0, here, :].astype(WIDE)).astype(LOW)

    def finish_gradient(i):
        here = pl.ds(pl.multiple_of(i * 16, 16), 16)
        xhat, rstd = standardize(tokens[here, :])
        scaled = landed[1, here, :].astype(WIDE) * gain[...]
        first = jnp.mean(scaled, axis=-1, keepdims=True)
        second = jnp.mean(scaled * xhat, axis=-1, keepdims=True)
        total = cot[here, :].astype(WIDE) + rstd * (scaled - first - xhat * second)
        ingrad_ref[here, :] = total.astype(LOW)

    landing(0)
    loop(rows // 16, finish_output)
    z_final(1, 0)
    z_final(1, 1)
    landing(1)
    loop(rows // 16, finish_gradient)

    @pl.when(place.home)
    def _():
        for c in range(2):
            for way in range(2):
                ya(1, way, 1, c).wait_recv()
            hand(1, 3, c)
        for c in range(2):
            for i in range(3):
                xa_came(0, i, c).wait_recv()
                hand(0, 1 + i, c)

    @pl.when(place.away)
    def _():
        for s, c in pieces:
            for i in range(4):
                hand_pair(s, i, c).wait_recv()
            xa(s, 0, c).wait_send()
            xa(s, 1, c).wait_send()
        for a, q in both:
            swap(a, q).wait_send()
            swap_back(a, q).wait_send()
        for i, h in weights:
            weight_swap(i, h).wait_send()

    @pl.when(place.home)
    def _():
        for s, c in pieces:
            for i in range(4):
                hand_pair(s, i, c).wait_send()
                hand_out(s, i, c).wait()
            xa(s, 2, c).wait_send()
        for way, k in both:
            for c in range(2):
                ya(1, way, k, c).wait_send()

    for a in range(2):
        for q in range(2):
            own_pair(a, q).wait_send()
        for way, k, q in hop_list:
            gather(a, way, k, q).wait_send()
            to_pair(a, way, k, q).wait_send()
        for j in order:
            core_copy(a, j).wait_send()
        for way, k, q in send_list:
            ring(a, way, k, q).wait_send()
    for way, k in both:
        for c in range(2):
            ya(0, way, k, c).wait_send()
            for s in range(2):
                f_copy(s, way, k, c).wait_send()
                s_copy(s, way, k, c).wait_send()


def run_layer(tokens, gain, w_qkv, w_out, cotangent):
    rows, dim = tokens.shape
    vmem = pl.BlockSpec(memory_space=pltpu.VMEM)
    any_space = pl.BlockSpec(memory_space=pl.ANY)
    dma = pltpu.SemaphoreType.DMA
    sums = 4 * w_out.shape[0]
    quarter = dim // 4

    def low(*shape):
        return pltpu.VMEM(shape, LOW)

    return pl.pallas_call(
        layer_kernel,
        out_shape=(
            jax.ShapeDtypeStruct((rows, dim), LOW),
            jax.ShapeDtypeStruct((rows, dim), LOW),
            jax.ShapeDtypeStruct((sums, dim), LOW),
        ),
        in_specs=[vmem, vmem, any_space, any_space, vmem],
        out_specs=(vmem, vmem, any_space),
        scratch_shapes=[
            low(rows, dim),
            low(rows * 16, dim),
            low(rows * 16, dim),
            low(6 * PAD, dim),
            low(2 * PAD, dim),
            low(rows * 16, 6 * PAD),
            low(rows * 16, 2 * PAD),
            low(rows * 16, 2 * PAD),
            low(rows * 16, 6 * PAD),
            pltpu.VMEM((4, LEN, LEN), WIDE),
            pltpu.VMEM((LEN, PAD), WIDE),
            pltpu.VMEM((LEN, PAD), WIDE),
            low(rows * 16, dim),
            low(rows * 16, dim),
            low(2, 8, rows, dim),
            low(2, rows, dim),
            low(2, 2, 3, rows, dim),
            low(2, rows, dim),
            low(2, rows, dim),
            low(sums, dim),
            low(2, 384, quarter),
            low(2, 2, 384, quarter),
            low(2, 384, quarter),
            low(2, 96, quarter),
            low(2, 2, 96, quarter),
            low(sums, dim),
            dma((2, 2)),
            dma((2, 2)),
            dma((2, 2)),
            dma((4, 2)),
            dma((4, 2)),
            dma((4, 2)),
            dma((2, 2, 4, 2)),
            dma((2, 2, 4, 2)),
            dma((2, 2)),
            dma((2, 2)),
            dma((2, 2, 4, 2)),
            dma((2, 2, 4, 2)),
            dma((2, 8)),
            dma((2, 8)),
            dma((2, 2, 4, 2)),
            dma((2, 2, 4, 2)),
            dma((2, 2)),
            dma((2, 2)),
            dma((2, 2)),
            dma((2, 2, 2, 2)),
            dma((2, 2, 2, 2)),
            dma((2, 2, 2, 2)),
            dma((2, 2, 2, 2)),
            dma((2, 2, 2, 2)),
            dma((2, 2, 2, 2)),
            dma((2, 3, 2)),
            dma((2, 3, 2)),
            dma((2, 4, 2)),
            dma((2, 4, 2)),
            dma((2, 4, 2)),
        ],
        compiler_params=pltpu.CompilerParams(
            collective_id=0, has_side_effects=True, vmem_limit_bytes=VMEM_BYTES
        ),
        name="attention_layer",
    )(tokens, gain.reshape(1, dim), w_qkv, w_out, cotangent)


def per_device(tokens, gain, w_qkv, w_out, cotangent):
    width = w_out.shape[0]
    output, input_gradient, sums = run_layer(tokens, gain, w_qkv, w_out, cotangent)
    replicas = lax.axis_size("dp")
    grad_qkv = sums[: 3 * width].astype(jnp.float32) / replicas
    grad_out = sums[3 * width :].astype(jnp.float32) / replicas
    return (output, input_gradient, grad_qkv.reshape(w_qkv.shape), grad_out)


def solution(mesh):
    placed = (
        P(("dp", "tensor"), None),
        P(),
        P(None, "tensor", None),
        P("tensor", None),
        P(("dp", "tensor"), None),
    )
    return jax.shard_map(
        per_device,
        mesh=mesh,
        in_specs=placed,
        out_specs=(
            P(("dp", "tensor"), None),
            P(("dp", "tensor"), None),
            P(None, "tensor", None),
            P("tensor", None),
        ),
        check_vma=False,
    )
```

```python
import jax
import jax.numpy as jnp
from jax import lax
from jax.experimental import pallas as pl
from jax.experimental.pallas import tpu as pltpu
from jax.sharding import PartitionSpec as P

HEAD_DIM = 80
LEN = 512
PAD = 128
BLOCK = 64
SCALE = HEAD_DIM ** (-0.5)
MESH = pl.DeviceIdType.MESH
VMEM_BYTES = 60 * 1024 * 1024
LOW = jnp.bfloat16
WIDE = jnp.float32


class Place:
    def __init__(self):
        dp, tensor = lax.axis_index("dp"), lax.axis_index("tensor")
        self.core = dp % 2
        self.y = (dp // 2) % 4
        self.x_lo = tensor % 2
        self.x = (dp // 8) * 2 + self.x_lo
        self.z = tensor // 2
        self.home = self.core == self.x_lo
        self.away = self.core != self.x_lo

    def at(self, x=None, y=None, z=None, core=None):
        x = self.x if x is None else x
        y = self.y if y is None else y
        z = self.z if z is None else z
        core = self.core if core is None else core
        return ((x // 2) * 8 + y * 2 + core, z * 2 + x % 2)

    def pair(self):
        return self.at(core=1 - self.core)

    def crossed(self, by, z_by=0):
        x, z = (self.x + by + 4) % 4, (self.z + z_by + 8) % 8
        return self.at(x=x, z=z, core=1 - self.core)

    def partner(self, z_by=0):
        return self.crossed(1 - 2 * self.x_lo, z_by)

    def z_next(self, by):
        return self.at(z=(self.z + by + 8) % 8)

    def x_next(self, by):
        return self.at(x=(self.x + by + 4) % 4)

    def y_next(self, by):
        return self.at(y=(self.y + by + 4) % 4)


def greet(devices):
    barrier = pltpu.get_barrier_semaphore()
    for device in devices:
        pl.semaphore_signal(barrier, inc=1, device_id=device, device_id_type=MESH)


def met(count):
    pl.semaphore_wait(pltpu.get_barrier_semaphore(), count)


def remote(source, target, send_sem, recv_sem, device):
    return pltpu.make_async_remote_copy(
        src_ref=source,
        dst_ref=target,
        send_sem=send_sem,
        recv_sem=recv_sem,
        device_id=device,
        device_id_type=MESH,
    )


def sum_into(target, terms):
    def step(i, carry):
        here = pl.ds(pl.multiple_of(i * 16, 16), 16)
        total = terms[0][here, :].astype(jnp.float32)
        for term in terms[1:]:
            total = total + term[here, :].astype(jnp.float32)
        target[here, :] = total.astype(jnp.bfloat16)
        return carry

    lax.fori_loop(0, target.shape[0] // 16, step, 0)


def nt(left, right):
    return lax.dot_general(left, right, (((1,), (1,)), ((), ())), preferred_element_type=WIDE)


def tn(left, right):
    return lax.dot_general(left, right, (((0,), (0,)), ((), ())), preferred_element_type=WIDE)


def nn(left, right):
    return jnp.dot(left, right, preferred_element_type=WIDE)


def standardize(x):
    xf = x.astype(WIDE)
    centered = xf - jnp.mean(xf, axis=-1, keepdims=True)
    var = jnp.mean(centered * centered, axis=-1, keepdims=True)
    rstd = lax.rsqrt(var + 1e-05)
    return centered * rstd, rstd


def loop(count, body):
    def step(i, carry):
        body(i)
        return carry

    lax.fori_loop(0, count, step, 0)


def layer_kernel(
    tokens,
    gain,
    wq_ref,
    wo_ref,
    cot,
    out_ref,
    ingrad_ref,
    g_out,
    stage,
    x_full,
    c_full,
    wq,
    wo,
    qkv,
    att,
    datt,
    dqkv,
    probs,
    dk_sum,
    dv_sum,
    parts,
    backs,
    theirs,
    first_buf,
    ring_buf,
    final,
    landed,
    g,
    f_first,
    f_buf,
    e_sum,
    s_first,
    s_buf,
    g_work,
    local_sem,
    swap_send,
    swap_recv,
    w_local,
    w_send,
    w_recv,
    gr_send,
    gr_recv,
    go_pair_send,
    go_pair_recv,
    gp_send,
    gp_recv,
    core_send,
    core_recv,
    ring_send,
    ring_recv,
    back_send,
    back_recv,
    back_local,
    f_send,
    f_recv,
    s_send,
    s_recv,
    ga_send,
    ga_recv,
    gh_send,
    gh_recv,
    go_send,
    go_recv,
    go_local,
    relay_send,
    relay_recv,
):
    place = Place()
    x, y, z, core = place.x, place.y, place.z, place.core
    dim = tokens.shape[1]
    rows = BLOCK
    half = rows // 2
    up, down = place.z_next(1), place.z_next(-1)
    pair, partner = place.pair(), place.partner()
    slant_up, slant_down = place.partner(1), place.partner(-1)
    right, left, across = place.x_next(1), place.x_next(-1), place.x_next(2)
    north, south = place.y_next(1), place.y_next(-1)
    cross_right, cross_left = place.crossed(1), place.crossed(-1)

    others = [up, down, pair, cross_right, cross_left, right, left, across, north, south]
    others += [slant_up, slant_down]
    greet(others)

    for i in range(6):
        wq[i * PAD + HEAD_DIM : (i + 1) * PAD, :] = jnp.zeros((PAD - HEAD_DIM, dim), LOW)
    for i in range(2):
        wo[i * PAD + HEAD_DIM : (i + 1) * PAD, :] = jnp.zeros((PAD - HEAD_DIM, dim), LOW)

    def norm_rows(i):
        here = pl.ds(pl.multiple_of(i * 16, 16), 16)
        xhat, _ = standardize(tokens[here, :])
        stage[here, :] = (xhat * gain[...].reshape(1, dim)).astype(LOW)

    loop(rows // 16, norm_rows)
    met(len(others))

    def block(full, owner, side, first=0, count=rows):
        owner = (owner + 8) % 8
        start = pl.multiple_of((owner * 2 + side) * rows + first, 32)
        return full.at[pl.ds(start, count), :]

    chunks = (slice(0, half), slice(half, rows))
    both = ((0, 0), (0, 1), (1, 0), (1, 1))
    fulls, owned = (x_full, c_full), (stage, cot)

    def hops(way, q):
        return 4 if way == q else 3

    def swap(a, q):
        target = block(fulls[a], z, 1 - core, q * half, half)
        source = owned[a].at[chunks[q], :]
        return remote(source, target, swap_send.at[a, q], swap_recv.at[a, q], partner)

    def keep(a, q):
        target = block(fulls[a], z, core, q * half, half)
        return pltpu.make_async_copy(owned[a].at[chunks[q], :], target, local_sem.at[a, q])

    def weight_ends(i, h):
        if i < 3:
            source = wq_ref.at[i, pl.ds(h * HEAD_DIM, HEAD_DIM), :]
            return source, wq.at[pl.ds((2 * i + h) * PAD, HEAD_DIM), :]
        return wo_ref.at[pl.ds(h * HEAD_DIM, HEAD_DIM), :], wo.at[pl.ds(h * PAD, HEAD_DIM), :]

    def weight_swap(i, h):
        device = cross_right if h == 0 else cross_left
        return remote(*weight_ends(i, h), w_send.at[i, h], w_recv.at[i, h], device)

    def weight_keep(i, h):
        return pltpu.make_async_copy(*weight_ends(i, h), w_local.at[i, h])

    weights = [(i, h) for i in range(4) for h in range(2)]

    def first_hop(way, q, crossing):
        side = 1 - core if crossing else core
        ends = (slant_up, slant_down) if crossing else (up, down)
        return remote(
            stage.at[chunks[q], :],
            block(x_full, z, side, q * half, half),
            gr_send.at[0, way, 0, q],
            gr_recv.at[0, way, 0, q],
            ends[way],
        )

    @pl.when(place.away)
    def _():
        for q in range(2):
            for way in range(2):
                first_hop(way, q, True).start()
            swap(0, q).start()
        for q in range(2):
            swap(1, q).start()
        for i, h in weights:
            weight_swap(i, h).start()

    @pl.when(place.home)
    def _():
        for q in range(2):
            for way in range(2):
                first_hop(way, q, False).start()
        for a, q in both:
            keep(a, q).start()
        for i, h in weights:
            weight_keep(i, h).start()

    def gather_piece(a, way, hop, q):
        return block(fulls[a], z - hop if way == 0 else z + hop, core, q * half, half)

    def gather(a, way, k, q):
        piece = gather_piece(a, way, k, q)
        device = up if way == 0 else down
        return remote(piece, piece, gr_send.at[a, way, k, q], gr_recv.at[a, way, k, q], device)

    def own_pair(a, q):
        piece = gather_piece(a, 0, 0, q)
        return remote(piece, piece, go_pair_send.at[a, q], go_pair_recv.at[a, q], pair)

    def to_pair(a, way, k, q):
        piece = gather_piece(a, way, k + 1, q)
        return remote(piece, piece, gp_send.at[a, way, k, q], gp_recv.at[a, way, k, q], pair)

    def begin(a, q):
        @pl.when(place.away)
        def _():
            swap(a, q).wait_recv()

        @pl.when(place.home)
        def _():
            keep(a, q).wait()

        if a == 1:
            for way in range(2):
                gather(a, way, 0, q).start()
        own_pair(a, q).start()

    def advance(a, k, q):
        for way in range(2):
            if k < hops(way, q):
                gather(a, way, k, q).wait_recv()
                if k + 1 < hops(way, q):
                    gather(a, way, k + 1, q).start()
                to_pair(a, way, k, q).start()

    hop_list = [(way, k, q) for k in range(4) for q in range(2) for way in range(2) if k < hops(way, q)]

    def gathered(a):
        for q in range(2):
            own_pair(a, q).wait_recv()
        for way, k, q in hop_list:
            to_pair(a, way, k, q).wait_recv()

    for q in range(2):
        begin(0, q)
    for k in range(3):
        for q in range(2):
            advance(0, k, q)
    for q in range(2):
        begin(1, q)
    for q in range(2):
        advance(0, 3, q)

    @pl.when(place.away)
    def _():
        for i, h in weights:
            weight_swap(i, h).wait_recv()

    @pl.when(place.home)
    def _():
        for i, h in weights:
            weight_keep(i, h).wait()

    gathered(0)

    def project(j):
        here = pl.ds(pl.multiple_of(j * 256, 256), 256)
        for i in range(3):
            cols = slice(i * 256, (i + 1) * 256)
            qkv[here, cols] = nt(x_full[here, :], wq[cols, :]).astype(LOW)

    def spots(u):
        r0 = pl.multiple_of((u // 2) * LEN, LEN)
        c0 = pl.multiple_of((u % 2) * PAD, PAD)
        return r0, c0

    def forward(u):
        r0, c0 = spots(u)
        for i in range(4):
            n = (i + 1) * 128
            here = pl.ds(r0 + i * 128, 128)
            query = qkv[here, pl.ds(c0, PAD)]
            key = qkv[pl.ds(r0, n), pl.ds(c0 + 256, PAD)]
            value = qkv[pl.ds(r0, n), pl.ds(c0 + 512, PAD)]
            scores = nt(query, key) * SCALE
            q_at = lax.broadcasted_iota(jnp.int32, (128, n), 0) + i * 128
            k_at = lax.broadcasted_iota(jnp.int32, (128, n), 1)
            scores = jnp.where(q_at >= k_at, scores, -1e30)
            expo = jnp.exp(scores - jnp.max(scores, axis=-1, keepdims=True))
            p = expo * (1.0 / jnp.sum(expo, axis=-1, keepdims=True))
            probs[u, i * 128 : (i + 1) * 128, :n] = p
            att[here, pl.ds(c0, PAD)] = nn(p.astype(LOW), value).astype(LOW)

    def one(at, body):
        loop(1, lambda i: body(at + i))

    def two(first, body):
        loop(2, lambda i: body(first + i))

    def out_parts(j):
        here = pl.ds(pl.multiple_of(j * 256, 256), 256)
        for i in range(10):
            cols = slice(i * 256, (i + 1) * 256)
            parts[here, cols] = nn(att[here, :], wo[:, cols]).astype(LOW)

    sources = (parts, backs)
    near = ((z + 4) % 8) // 2
    groups = (near, (near + 1) % 4, (near + 3) % 4, (near + 2) % 4)
    order = (4, 3, -3, 2, -2, 1, -1, 0)

    def core_copy(a, j):
        owner = (z + j + 8) % 8
        source = block(sources[a], owner, 1 - core)
        return remote(
            source, theirs.at[a, owner], core_send.at[a, j + 3], core_recv.at[a, j + 3], pair
        )

    def ring(a, way, k, q):
        sign = 1 if way == 0 else -1
        owner = (z + sign * (4 - k) + 8) % 8
        source = theirs.at[a, owner, chunks[q], :]
        if k == 0:
            target = first_buf.at[a, chunks[q], :]
        else:
            target = ring_buf.at[a, way, k - 1, chunks[q], :]
        device = up if way == 0 else down
        return remote(source, target, ring_send.at[a, way, k, q], ring_recv.at[a, way, k, q], device)

    def z_step(a, k, q):
        for way in range(2):
            if k < 4 - hops(way, q):
                continue
            j = (4 - k) * (1 if way == 0 else -1)
            owner = (z + j + 8) % 8
            own = block(sources[a], owner, core, q * half, half)
            other = theirs.at[a, owner, chunks[q], :]
            terms = [own, other]
            if k == 0:
                if q == 0:
                    core_copy(a, 4).wait_recv()
            else:
                if q == 0:
                    core_copy(a, j).wait_recv()
                if k > 4 - hops(way, q):
                    ring(a, way, k - 1, q).wait_recv()
                    if k == 1:
                        terms.append(first_buf.at[a, chunks[q], :])
                    else:
                        terms.append(ring_buf.at[a, way, k - 2, chunks[q], :])
            sum_into(other, terms)
            ring(a, way, k, q).start()

    send_list = [(way, k, q) for k in range(4) for q in range(2) for way in range(2) if k >= 4 - hops(way, q)]

    def swap_back(a, q):
        source, target = final.at[a, chunks[q], :], landed.at[a, chunks[q], :]
        return remote(source, target, back_send.at[a, q], back_recv.at[a, q], partner)

    def keep_back(a, q):
        source, target = final.at[a, chunks[q], :], landed.at[a, chunks[q], :]
        return pltpu.make_async_copy(source, target, back_local.at[a, q])

    def z_final(a, q):
        if q == 0:
            core_copy(a, 0).wait_recv()
        terms = [block(sources[a], z, core, q * half, half), theirs.at[a, z, chunks[q], :]]
        for way in range(2):
            ring(a, way, 3, q).wait_recv()
            terms.append(ring_buf.at[a, way, 2, chunks[q], :])
        sum_into(final.at[a, chunks[q], :], terms)

        @pl.when(place.away)
        def _():
            swap_back(a, q).start()

        @pl.when(place.home)
        def _():
            keep_back(a, q).start()

    def core_copies(a, js):
        for j in js:
            core_copy(a, j).start()

    one(0, project)
    advance(1, 0, 0)
    one(1, project)
    advance(1, 0, 1)
    one(2, project)
    advance(1, 1, 0)
    one(3, project)
    advance(1, 1, 1)
    one(0, forward)
    one(1, forward)
    advance(1, 2, 0)
    one(2, forward)
    one(3, forward)
    advance(1, 2, 1)
    one(groups[0], out_parts)
    core_copies(0, (4,))
    one(groups[1], out_parts)
    one(groups[2], out_parts)
    core_copies(0, (3, -3, 2, -2))
    z_step(0, 0, 0)
    z_step(0, 0, 1)
    one(groups[3], out_parts)
    core_copies(0, (1, -1, 0))
    advance(1, 3, 0)
    advance(1, 3, 1)
    gathered(1)

    def project_back(j):
        here = pl.ds(pl.multiple_of(j * 256, 256), 256)
        datt[here, :] = nt(c_full[here, :], wo[...]).astype(LOW)

    def backward(u):
        r0, c0 = spots(u)
        for i in (3, 2, 1, 0):
            n = (i + 1) * 128
            here = pl.ds(r0 + i * 128, 128)
            query = qkv[here, pl.ds(c0, PAD)]
            key = qkv[pl.ds(r0, n), pl.ds(c0 + 256, PAD)]
            value = qkv[pl.ds(r0, n), pl.ds(c0 + 512, PAD)]
            d_att = datt[here, pl.ds(c0, PAD)]
            p = probs[u, i * 128 : (i + 1) * 128, :n]
            d_probs = nt(d_att, value)
            d_score = p * (d_probs - jnp.sum(d_probs * p, axis=-1, keepdims=True)) * SCALE
            d_low = d_score.astype(LOW)
            dqkv[here, pl.ds(c0, PAD)] = nn(d_low, key).astype(LOW)
            dk, dv = tn(d_low, query), tn(p.astype(LOW), d_att)
            if i == 3:
                dk_sum[...] = dk
                dv_sum[...] = dv
            else:
                dk_sum[:n, :] += dk
                dv_sum[:n, :] += dv
        dqkv[pl.ds(r0, LEN), pl.ds(c0 + 256, PAD)] = dk_sum[...].astype(LOW)
        dqkv[pl.ds(r0, LEN), pl.ds(c0 + 512, PAD)] = dv_sum[...].astype(LOW)

    loop(4, project_back)
    z_step(0, 1, 0)
    one(0, backward)
    z_step(0, 1, 1)
    two(1, backward)
    z_step(0, 2, 0)
    one(3, backward)

    def turn(i):
        for j in range(4):
            cut = slice(j * 256, (j + 1) * 256)
            source = dqkv[cut, i * 256 : (i + 1) * 256] if i < 3 else att[cut, :]
            backs[i * 256 : (i + 1) * 256, cut] = source.T

    def weight_grads(s, q):
        for i in (2 * s, 2 * s + 1):
            factor = backs[i * 256 : (i + 1) * 256, 0:1024]
            total = nn(factor, (x_full if i < 3 else c_full)[:, columns(q)]).astype(LOW)
            for h in range(2):
                spot = i * 160 + h * HEAD_DIM
                g[spot : spot + HEAD_DIM, columns(q)] = total[h * PAD : h * PAD + HEAD_DIM, :]

    side_start, side_rows, subs, width = (0, 320), (320, 320), (80, 80), dim // 4
    firsts, seconds = (x, y), (y, x)
    neighbours = ((right, left), (north, south))
    lanes = (slice(0, 384), slice(384, 640))
    pieces = [(s, c) for c in range(2) for s in range(2)]

    def half_of(s, way, size):
        count = (size[s] // 16 + 1) // 2 * 16
        return slice(0, count) if way == 0 else slice(count, size[s])

    def columns(q):
        return pl.ds(pl.multiple_of(((q + 4) % 4) * width, 128), width)

    def g_side(s, q, c):
        return g.at[pl.ds(side_start[s], side_rows[s]), columns(q)].at[:, lanes[c]]

    def sub_rows(s, q):
        return pl.ds(pl.multiple_of(((q + 4) % 4) * subs[s], 16), subs[s])

    def e_sub(s, q, c):
        return e_sum.at[s, sub_rows(s, q), lanes[c]]

    def step_to(s, way, places):
        return places[s] + (1 if way == 0 else -1)

    def f_copy(s, way, k, c):
        device = neighbours[s][way]
        sems = (f_send.at[s, way, k, c], f_recv.at[s, way, k, c])
        if k == 0:
            part = half_of(s, way, side_rows)
            source = g_side(s, firsts[s] + 2, c).at[part, :]
            return remote(source, f_first.at[s, part, lanes[c]], *sems, device)
        source = g_side(s, step_to(s, way, firsts), c)
        return remote(source, f_buf.at[s, way, 0 : side_rows[s], lanes[c]], *sems, device)

    def s_copy(s, way, k, c):
        device = neighbours[1 - s][way]
        sems = (s_send.at[s, way, k, c], s_recv.at[s, way, k, c])
        if k == 0:
            part = half_of(s, way, subs)
            source = e_sub(s, seconds[s] + 2, c).at[part, :]
            return remote(source, s_first.at[s, part, lanes[c]], *sems, device)
        source = e_sub(s, step_to(s, way, seconds), c)
        return remote(source, s_buf.at[s, way, 0 : subs[s], lanes[c]], *sems, device)

    def f_pass(s, c):
        for way in range(2):
            f_copy(s, way, 0, c).wait_recv()
            part = half_of(s, way, side_rows)
            own = g_side(s, step_to(s, way, firsts), c).at[part, :]
            sum_into(own, [own, f_first.at[s, part, lanes[c]]])
            f_copy(s, way, 1, c).start()

    def f_final(s, c):
        for way in range(2):
            f_copy(s, way, 1, c).wait_recv()
        came = [f_buf.at[s, way, 0 : side_rows[s], lanes[c]] for way in range(2)]
        sum_into(e_sum.at[s, 0 : side_rows[s], lanes[c]], [g_side(s, firsts[s], c)] + came)
        for way in range(2):
            s_copy(s, way, 0, c).start()

    def s_pass(s, c):
        for way in range(2):
            s_copy(s, way, 0, c).wait_recv()
            part = half_of(s, way, subs)
            own = e_sub(s, step_to(s, way, seconds), c).at[part, :]
            sum_into(own, [own, s_first.at[s, part, lanes[c]]])
            s_copy(s, way, 1, c).start()

    def work(s, row, col, c):
        start = pl.multiple_of(side_start[s] + ((row + 4) % 4) * subs[s], 16)
        return g_work.at[pl.ds(start, subs[s]), columns(col)].at[:, lanes[c]]

    def work_column(s, col, c):
        return g_work.at[pl.ds(side_start[s], side_rows[s]), columns(col)].at[:, lanes[c]]

    def s_final(s, c):
        for way in range(2):
            s_copy(s, way, 1, c).wait_recv()
        came = [s_buf.at[s, way, 0 : subs[s], lanes[c]] for way in range(2)]
        sum_into(work(s, seconds[s], firsts[s], c), [e_sub(s, seconds[s], c)] + came)

    def ya(s, way, k, c):
        device = north if way == 0 else south
        at = y if k == 0 else (y - 1 if way == 0 else y + 1)
        if s == 0:
            spot, size = work(0, at, x, c), subs
        else:
            spot, size = work_column(1, at, c), side_rows
        if k == 1:
            spot = spot.at[half_of(s, way, size), :]
        return remote(spot, spot, ga_send.at[s, way, k, c], ga_recv.at[s, way, k, c], device)

    def xa(s, i, c):
        spot = work_column(0, x, c) if s == 0 else work(1, x, y, c)
        device = (right, left, across)[i]
        return remote(spot, spot, gh_send.at[s, i, c], gh_recv.at[s, i, c], device)

    def xa_came(s, i, c):
        source = (x - 1, x + 1, x + 2)[i]
        spot = work_column(0, source, c) if s == 0 else work(1, source, y, c)
        return remote(spot, spot, gh_send.at[s, i, c], gh_recv.at[s, i, c], pair)

    relay_in = remote(
        work_column(0, x, 1), work_column(0, x, 1), relay_send, relay_recv, left
    )
    relay_out = remote(
        work_column(0, x + 1, 1),
        work_column(0, x + 1, 1),
        gh_send.at[0, 2, 1],
        gh_recv.at[0, 2, 1],
        left,
    )

    def xa_start(s, c):
        @pl.when(place.away)
        def _():
            xa(s, 0, c).start()
            xa(s, 1, c).start()

        @pl.when(place.home)
        def _():
            if (s, c) == (0, 1):
                relay_in.start()
            else:
                xa(s, 2, c).start()

    def handed(s, i, c):
        at = x if s == 0 else y
        place_of = columns((at, at - 1, at + 1, at + 2)[i])
        return lambda ref: ref.at[pl.ds(side_start[s], side_rows[s]), place_of].at[:, lanes[c]]

    def hand_pair(s, i, c):
        spot = handed(s, i, c)
        return remote(spot(g_work), spot(g_out), go_send.at[s, i, c], go_recv.at[s, i, c], pair)

    def hand_out(s, i, c):
        spot = handed(s, i, c)
        return pltpu.make_async_copy(spot(g_work), spot(g_out), go_local.at[s, i, c])

    def hand(s, i, c):
        hand_pair(s, i, c).start()
        hand_out(s, i, c).start()

    def y_start(c):
        for way in range(2):
            ya(0, way, 0, c).start()
        xa_start(1, c)

    def y_pass(c):
        for way in range(2):
            ya(0, way, 0, c).wait_recv()
            ya(0, way, 1, c).start()

    def y_final(c):
        for way in range(2):
            ya(0, way, 1, c).wait_recv()
        xa_start(0, c)

    def f_start(s):
        for c in range(2):
            for way in range(2):
                f_copy(s, way, 0, c).start()

    turn(0)
    turn(1)
    weight_grads(0, x + 2)
    f_start(0)
    z_step(0, 2, 1)
    turn(2)
    turn(3)
    weight_grads(1, y + 2)
    f_start(1)
    weight_grads(0, x + 1)
    weight_grads(0, x - 1)
    f_pass(0, 0)
    f_pass(0, 1)
    z_step(0, 3, 0)
    weight_grads(1, y + 1)
    weight_grads(1, y - 1)
    f_pass(1, 0)
    f_pass(1, 1)
    z_step(0, 3, 1)
    weight_grads(0, x)
    weight_grads(1, y)

    def back_parts(j):
        here = pl.ds(pl.multiple_of(j * 256, 256), 256)
        for i in range(10):
            cols = slice(i * 256, (i + 1) * 256)
            backs[here, cols] = nn(dqkv[here, :], wq[:, cols]).astype(LOW)

    one(groups[0], back_parts)
    core_copies(1, (4,))
    one(groups[1], back_parts)
    z_step(1, 0, 0)
    z_step(1, 0, 1)
    one(groups[2], back_parts)
    core_copies(1, (3, -3, 2, -2))
    f_final(0, 0)
    z_final(0, 0)
    z_step(1, 1, 0)
    one(groups[3], back_parts)
    core_copies(1, (1, -1, 0))
    z_final(0, 1)
    z_step(1, 1, 1)
    f_final(1, 0)
    z_step(1, 2, 0)
    s_pass(0, 0)
    s_pass(1, 0)
    f_final(0, 1)
    f_final(1, 1)
    z_step(1, 2, 1)
    s_pass(0, 1)
    s_pass(1, 1)
    s_final(0, 0)
    s_final(1, 0)
    y_start(0)
    z_step(1, 3, 0)
    s_final(0, 1)
    s_final(1, 1)
    y_start(1)
    y_pass(0)
    z_step(1, 3, 1)
    y_pass(1)
    y_final(0)

    @pl.when(place.home)
    def _():
        for c in range(2):
            for i in range(3):
                xa_came(1, i, c).wait_recv()
            for way in range(2):
                ya(1, way, 0, c).start()
            hand(1, 0, c)
            if c == 0:
                hand(0, 0, 0)

    y_final(1)

    @pl.when(place.home)
    def _():
        hand(0, 0, 1)
        for c in range(2):
            for way in range(2):
                ya(1, way, 0, c).wait_recv()
                ya(1, way, 1, c).start()
                hand(1, 1 + way, c)

    def landing(a):
        @pl.when(place.away)
        def _():
            for q in range(2):
                swap_back(a, q).wait_recv()

        @pl.when(place.home)
        def _():
            for q in range(2):
                keep_back(a, q).wait()

    def finish_output(i):
        here = pl.ds(pl.multiple_of(i * 16, 16), 16)
        out_ref[here, :] = (tokens[here, :].astype(WIDE) + landed[0, here, :].astype(WIDE)).astype(LOW)

    def finish_gradient(i):
        here = pl.ds(pl.multiple_of(i * 16, 16), 16)
        xhat, rstd = standardize(tokens[here, :])
        scaled = landed[1, here, :].astype(WIDE) * gain[...].reshape(1, dim)
        first = jnp.mean(scaled, axis=-1, keepdims=True)
        second = jnp.mean(scaled * xhat, axis=-1, keepdims=True)
        total = cot[here, :].astype(WIDE) + rstd * (scaled - first - xhat * second)
        ingrad_ref[here, :] = total.astype(LOW)

    landing(0)
    loop(rows // 16, finish_output)
    z_final(1, 0)
    z_final(1, 1)
    @pl.when(place.away)
    def _():
        relay_in.wait_recv()
        relay_out.start()

    landing(1)
    loop(rows // 16, finish_gradient)

    @pl.when(place.home)
    def _():
        for c in range(2):
            for way in range(2):
                ya(1, way, 1, c).wait_recv()
            hand(1, 3, c)
        for c in range(2):
            for i in range(3):
                xa_came(0, i, c).wait_recv()
                hand(0, 1 + i, c)

    @pl.when(place.away)
    def _():
        for s, c in pieces:
            for i in range(4):
                hand_pair(s, i, c).wait_recv()
            xa(s, 0, c).wait_send()
            xa(s, 1, c).wait_send()
        relay_out.wait_send()
        for a, q in both:
            swap(a, q).wait_send()
            swap_back(a, q).wait_send()
        for i, h in weights:
            weight_swap(i, h).wait_send()

    @pl.when(place.home)
    def _():
        for s, c in pieces:
            for i in range(4):
                hand_pair(s, i, c).wait_send()
                hand_out(s, i, c).wait()
            if (s, c) == (0, 1):
                relay_in.wait_send()
            else:
                xa(s, 2, c).wait_send()
        for way, k in both:
            for c in range(2):
                ya(1, way, k, c).wait_send()

    for a in range(2):
        for q in range(2):
            own_pair(a, q).wait_send()
        for way, k, q in hop_list:
            gather(a, way, k, q).wait_send()
            to_pair(a, way, k, q).wait_send()
        for j in order:
            core_copy(a, j).wait_send()
        for way, k, q in send_list:
            ring(a, way, k, q).wait_send()
    for way, k in both:
        for c in range(2):
            ya(0, way, k, c).wait_send()
            for s in range(2):
                f_copy(s, way, k, c).wait_send()
                s_copy(s, way, k, c).wait_send()


def run_layer(tokens, gain, w_qkv, w_out, cotangent):
    rows, dim = tokens.shape
    vmem = pl.BlockSpec(memory_space=pltpu.VMEM)
    any_space = pl.BlockSpec(memory_space=pl.ANY)
    dma = pltpu.SemaphoreType.DMA
    sums = 4 * w_out.shape[0]
    quarter = dim // 4

    def low(*shape):
        return pltpu.VMEM(shape, LOW)

    return pl.pallas_call(
        layer_kernel,
        out_shape=(
            jax.ShapeDtypeStruct((rows, dim), LOW),
            jax.ShapeDtypeStruct((rows, dim), LOW),
            jax.ShapeDtypeStruct((sums, dim), LOW),
        ),
        in_specs=[vmem, vmem, any_space, any_space, vmem],
        out_specs=(vmem, vmem, any_space),
        scratch_shapes=[
            low(rows, dim),
            low(rows * 16, dim),
            low(rows * 16, dim),
            low(6 * PAD, dim),
            low(2 * PAD, dim),
            low(rows * 16, 6 * PAD),
            low(rows * 16, 2 * PAD),
            low(rows * 16, 2 * PAD),
            low(rows * 16, 6 * PAD),
            pltpu.VMEM((4, LEN, LEN), WIDE),
            pltpu.VMEM((LEN, PAD), WIDE),
            pltpu.VMEM((LEN, PAD), WIDE),
            low(rows * 16, dim),
            low(rows * 16, dim),
            low(2, 8, rows, dim),
            low(2, rows, dim),
            low(2, 2, 3, rows, dim),
            low(2, rows, dim),
            low(2, rows, dim),
            low(sums, dim),
            low(2, 320, quarter),
            low(2, 2, 320, quarter),
            low(2, 320, quarter),
            low(2, 80, quarter),
            low(2, 2, 80, quarter),
            low(sums, dim),
            dma((2, 2)),
            dma((2, 2)),
            dma((2, 2)),
            dma((4, 2)),
            dma((4, 2)),
            dma((4, 2)),
            dma((2, 2, 4, 2)),
            dma((2, 2, 4, 2)),
            dma((2, 2)),
            dma((2, 2)),
            dma((2, 2, 4, 2)),
            dma((2, 2, 4, 2)),
            dma((2, 8)),
            dma((2, 8)),
            dma((2, 2, 4, 2)),
            dma((2, 2, 4, 2)),
            dma((2, 2)),
            dma((2, 2)),
            dma((2, 2)),
            dma((2, 2, 2, 2)),
            dma((2, 2, 2, 2)),
            dma((2, 2, 2, 2)),
            dma((2, 2, 2, 2)),
            dma((2, 2, 2, 2)),
            dma((2, 2, 2, 2)),
            dma((2, 3, 2)),
            dma((2, 3, 2)),
            dma((2, 4, 2)),
            dma((2, 4, 2)),
            dma((2, 4, 2)),
            dma,
            dma,
        ],
        compiler_params=pltpu.CompilerParams(
            collective_id=0, has_side_effects=True, vmem_limit_bytes=VMEM_BYTES
        ),
        name="attention_layer",
    )(tokens, gain, w_qkv, w_out, cotangent)


def widen_kernel(sums, out_in, ingrad_in, gq, go, out, ingrad, low_buf, wide_buf, in_sem, out_sem):
    count, split = 80, gq.shape[0]
    scale = 1.0 / lax.axis_size("dp")

    def fetch(i):
        spot = slice(i * count, (i + 1) * count)
        return pltpu.make_async_copy(sums.at[spot, :], low_buf.at[spot, :], in_sem.at[i])

    def store(i):
        first = i * count
        source = wide_buf.at[first : first + count, :]
        ref, at = (gq, first) if first < split else (go, first - split)
        return pltpu.make_async_copy(source, ref.at[at : at + count, :], out_sem.at[i])

    steps = sums.shape[0] // count
    for i in range(steps):
        fetch(i).start()
    out[...] = out_in[...]
    ingrad[...] = ingrad_in[...]
    for i in range(steps):
        fetch(i).wait()

        def widen(k):
            here = pl.ds(pl.multiple_of(i * count + k * 16, 16), 16)
            wide_buf[here, :] = low_buf[here, :].astype(WIDE) * scale

        loop(count // 16, widen)
        store(i).start()
    for i in range(steps):
        store(i).wait()


def widen_sums(sums, output, input_gradient, width):
    total, dim = sums.shape
    vmem = pl.BlockSpec(memory_space=pltpu.VMEM)
    any_space = pl.BlockSpec(memory_space=pl.ANY)
    return pl.pallas_call(
        widen_kernel,
        out_shape=(
            jax.ShapeDtypeStruct((3 * width, dim), WIDE),
            jax.ShapeDtypeStruct((total - 3 * width, dim), WIDE),
            jax.ShapeDtypeStruct(output.shape, LOW),
            jax.ShapeDtypeStruct(output.shape, LOW),
        ),
        in_specs=[any_space, vmem, vmem],
        out_specs=(any_space, any_space, vmem, vmem),
        scratch_shapes=[
            pltpu.VMEM((total, dim), LOW),
            pltpu.VMEM((total, dim), WIDE),
            pltpu.SemaphoreType.DMA((8,)),
            pltpu.SemaphoreType.DMA((8,)),
        ],
        compiler_params=pltpu.CompilerParams(vmem_limit_bytes=VMEM_BYTES),
        name="widen_sums",
    )(sums, output, input_gradient)


def per_device(tokens, gain, w_qkv, w_out, cotangent):
    width = w_out.shape[0]
    output, input_gradient, sums = run_layer(tokens, gain, w_qkv, w_out, cotangent)
    grad_qkv, grad_out, output, input_gradient = widen_sums(sums, output, input_gradient, width)
    return (output, input_gradient, grad_qkv.reshape(w_qkv.shape), grad_out)


def solution(mesh):
    placed = (
        P(("dp", "tensor"), None),
        P(),
        P(None, "tensor", None),
        P("tensor", None),
        P(("dp", "tensor"), None),
    )
    return jax.shard_map(
        per_device,
        mesh=mesh,
        in_specs=placed,
        out_specs=(
            P(("dp", "tensor"), None),
            P(("dp", "tensor"), None),
            P(None, "tensor", None),
            P("tensor", None),
        ),
        check_vma=False,
    )
```

```python
import jax
import jax.numpy as jnp
from jax import lax
from jax.experimental import pallas as pl
from jax.experimental.pallas import tpu as pltpu
from jax.sharding import PartitionSpec as P

HEAD_DIM = 80
LEN = 512
PAD = 128
BLOCK = 64
SCALE = HEAD_DIM ** (-0.5)
MESH = pl.DeviceIdType.MESH
VMEM_BYTES = 60 * 1024 * 1024
LOW = jnp.bfloat16
WIDE = jnp.float32


class Place:
    def __init__(self):
        dp, tensor = lax.axis_index("dp"), lax.axis_index("tensor")
        self.core = dp % 2
        self.y = (dp // 2) % 4
        self.x_lo = tensor % 2
        self.x = (dp // 8) * 2 + self.x_lo
        self.z = tensor // 2
        self.home = self.core == self.x_lo
        self.away = self.core != self.x_lo

    def at(self, x=None, y=None, z=None, core=None):
        x = self.x if x is None else x
        y = self.y if y is None else y
        z = self.z if z is None else z
        core = self.core if core is None else core
        return ((x // 2) * 8 + y * 2 + core, z * 2 + x % 2)

    def pair(self):
        return self.at(core=1 - self.core)

    def crossed(self, by, z_by=0):
        x, z = (self.x + by + 4) % 4, (self.z + z_by + 8) % 8
        return self.at(x=x, z=z, core=1 - self.core)

    def partner(self, z_by=0):
        return self.crossed(1 - 2 * self.x_lo, z_by)

    def z_next(self, by):
        return self.at(z=(self.z + by + 8) % 8)

    def x_next(self, by):
        return self.at(x=(self.x + by + 4) % 4)

    def y_next(self, by):
        return self.at(y=(self.y + by + 4) % 4)


def greet(devices):
    barrier = pltpu.get_barrier_semaphore()
    for device in devices:
        pl.semaphore_signal(barrier, inc=1, device_id=device, device_id_type=MESH)


def met(count):
    pl.semaphore_wait(pltpu.get_barrier_semaphore(), count)


def remote(source, target, send_sem, recv_sem, device):
    return pltpu.make_async_remote_copy(
        src_ref=source,
        dst_ref=target,
        send_sem=send_sem,
        recv_sem=recv_sem,
        device_id=device,
        device_id_type=MESH,
    )


def sum_into(target, terms):
    def step(i, carry):
        here = pl.ds(pl.multiple_of(i * 16, 16), 16)
        total = terms[0][here, :].astype(jnp.float32)
        for term in terms[1:]:
            total = total + term[here, :].astype(jnp.float32)
        target[here, :] = total.astype(jnp.bfloat16)
        return carry

    lax.fori_loop(0, target.shape[0] // 16, step, 0)


def nt(left, right):
    return lax.dot_general(left, right, (((1,), (1,)), ((), ())), preferred_element_type=WIDE)


def tn(left, right):
    return lax.dot_general(left, right, (((0,), (0,)), ((), ())), preferred_element_type=WIDE)


def nn(left, right):
    return jnp.dot(left, right, preferred_element_type=WIDE)


def standardize(x):
    xf = x.astype(WIDE)
    centered = xf - jnp.mean(xf, axis=-1, keepdims=True)
    var = jnp.mean(centered * centered, axis=-1, keepdims=True)
    rstd = lax.rsqrt(var + 1e-05)
    return centered * rstd, rstd


def loop(count, body):
    def step(i, carry):
        body(i)
        return carry

    lax.fori_loop(0, count, step, 0)


def layer_kernel(
    tokens,
    gain,
    wq_ref,
    wo_ref,
    cot,
    out_ref,
    ingrad_ref,
    g_out,
    stage,
    x_full,
    c_full,
    wq,
    wo,
    qkv,
    att,
    datt,
    dqkv,
    probs,
    dk_sum,
    dv_sum,
    parts,
    backs,
    theirs,
    first_buf,
    ring_buf,
    final,
    landed,
    g,
    f_first,
    f_buf,
    e_sum,
    s_first,
    s_buf,
    g_work,
    local_sem,
    swap_send,
    swap_recv,
    w_local,
    w_send,
    w_recv,
    gr_send,
    gr_recv,
    go_pair_send,
    go_pair_recv,
    gp_send,
    gp_recv,
    core_send,
    core_recv,
    ring_send,
    ring_recv,
    back_send,
    back_recv,
    back_local,
    f_send,
    f_recv,
    s_send,
    s_recv,
    ga_send,
    ga_recv,
    gh_send,
    gh_recv,
    go_send,
    go_recv,
    go_local,
    relay_send,
    relay_recv,
):
    place = Place()
    x, y, z, core = place.x, place.y, place.z, place.core
    dim = tokens.shape[1]
    rows = BLOCK
    half = rows // 2
    up, down = place.z_next(1), place.z_next(-1)
    pair, partner = place.pair(), place.partner()
    slant_up, slant_down = place.partner(1), place.partner(-1)
    right, left, across = place.x_next(1), place.x_next(-1), place.x_next(2)
    north, south = place.y_next(1), place.y_next(-1)
    cross_right, cross_left = place.crossed(1), place.crossed(-1)

    others = [up, down, pair, cross_right, cross_left, right, left, across, north, south]
    others += [slant_up, slant_down]
    greet(others)

    for i in range(6):
        wq[i * PAD + HEAD_DIM : (i + 1) * PAD, :] = jnp.zeros((PAD - HEAD_DIM, dim), LOW)
    for i in range(2):
        wo[i * PAD + HEAD_DIM : (i + 1) * PAD, :] = jnp.zeros((PAD - HEAD_DIM, dim), LOW)

    def norm_rows(i):
        here = pl.ds(pl.multiple_of(i * 32, 32), 32)
        xhat, _ = standardize(tokens[here, :])
        stage[here, :] = (xhat * gain[...].reshape(1, dim)).astype(LOW)

    loop(rows // 32, norm_rows)
    met(len(others))

    def block(full, owner, side, first=0, count=rows):
        owner = (owner + 8) % 8
        start = pl.multiple_of((owner * 2 + side) * rows + first, 32)
        return full.at[pl.ds(start, count), :]

    chunks = (slice(0, half), slice(half, rows))
    both = ((0, 0), (0, 1), (1, 0), (1, 1))
    fulls, owned = (x_full, c_full), (stage, cot)

    def hops(way, q):
        return 4 if way == q else 3

    def swap(a, q):
        target = block(fulls[a], z, 1 - core, q * half, half)
        source = owned[a].at[chunks[q], :]
        return remote(source, target, swap_send.at[a, q], swap_recv.at[a, q], partner)

    def keep(a, q):
        target = block(fulls[a], z, core, q * half, half)
        return pltpu.make_async_copy(owned[a].at[chunks[q], :], target, local_sem.at[a, q])

    def weight_ends(i, h):
        if i < 3:
            source = wq_ref.at[i, pl.ds(h * HEAD_DIM, HEAD_DIM), :]
            return source, wq.at[pl.ds((2 * i + h) * PAD, HEAD_DIM), :]
        return wo_ref.at[pl.ds(h * HEAD_DIM, HEAD_DIM), :], wo.at[pl.ds(h * PAD, HEAD_DIM), :]

    def weight_swap(i, h):
        device = cross_right if h == 0 else cross_left
        return remote(*weight_ends(i, h), w_send.at[i, h], w_recv.at[i, h], device)

    def weight_keep(i, h):
        return pltpu.make_async_copy(*weight_ends(i, h), w_local.at[i, h])

    weights = [(i, h) for i in range(4) for h in range(2)]

    def first_hop(way, q, crossing):
        side = 1 - core if crossing else core
        ends = (slant_up, slant_down) if crossing else (up, down)
        return remote(
            stage.at[chunks[q], :],
            block(x_full, z, side, q * half, half),
            gr_send.at[0, way, 0, q],
            gr_recv.at[0, way, 0, q],
            ends[way],
        )

    @pl.when(place.away)
    def _():
        for q in range(2):
            for way in range(2):
                first_hop(way, q, True).start()
            swap(0, q).start()
        for q in range(2):
            swap(1, q).start()
        for i, h in weights:
            weight_swap(i, h).start()

    @pl.when(place.home)
    def _():
        for q in range(2):
            for way in range(2):
                first_hop(way, q, False).start()
        for a, q in both:
            keep(a, q).start()
        for i, h in weights:
            weight_keep(i, h).start()

    def gather_piece(a, way, hop, q):
        return block(fulls[a], z - hop if way == 0 else z + hop, core, q * half, half)

    def gather(a, way, k, q):
        piece = gather_piece(a, way, k, q)
        device = up if way == 0 else down
        return remote(piece, piece, gr_send.at[a, way, k, q], gr_recv.at[a, way, k, q], device)

    def own_pair(a, q):
        piece = gather_piece(a, 0, 0, q)
        return remote(piece, piece, go_pair_send.at[a, q], go_pair_recv.at[a, q], pair)

    def to_pair(a, way, k, q):
        piece = gather_piece(a, way, k + 1, q)
        return remote(piece, piece, gp_send.at[a, way, k, q], gp_recv.at[a, way, k, q], pair)

    def begin(a, q):
        @pl.when(place.away)
        def _():
            swap(a, q).wait_recv()

        @pl.when(place.home)
        def _():
            keep(a, q).wait()

        if a == 1:
            for way in range(2):
                gather(a, way, 0, q).start()
        own_pair(a, q).start()

    def advance(a, k, q):
        for way in range(2):
            if k < hops(way, q):
                gather(a, way, k, q).wait_recv()
                if k + 1 < hops(way, q):
                    gather(a, way, k + 1, q).start()
                to_pair(a, way, k, q).start()

    hop_list = [(way, k, q) for k in range(4) for q in range(2) for way in range(2) if k < hops(way, q)]

    def gathered(a, hop_counts):
        if 0 in hop_counts:
            for q in range(2):
                own_pair(a, q).wait_recv()
        for way, k, q in hop_list:
            if k in hop_counts:
                to_pair(a, way, k, q).wait_recv()

    for q in range(2):
        begin(0, q)
    for k in range(3):
        for q in range(2):
            advance(0, k, q)
    for q in range(2):
        begin(1, q)
    for q in range(2):
        advance(0, 3, q)

    @pl.when(place.away)
    def _():
        for i, h in weights:
            weight_swap(i, h).wait_recv()

    @pl.when(place.home)
    def _():
        for i, h in weights:
            weight_keep(i, h).wait()

    gathered(0, range(4))

    def project(j):
        here = pl.ds(pl.multiple_of(j * 256, 256), 256)
        for i in range(3):
            cols = slice(i * 256, (i + 1) * 256)
            qkv[here, cols] = nt(x_full[here, :], wq[cols, :]).astype(LOW)

    def spots(u):
        r0 = pl.multiple_of((u // 2) * LEN, LEN)
        c0 = pl.multiple_of((u % 2) * PAD, PAD)
        return r0, c0

    def forward(u):
        r0, c0 = spots(u)
        for i in range(4):
            n = (i + 1) * 128
            here = pl.ds(r0 + i * 128, 128)
            query = qkv[here, pl.ds(c0, PAD)]
            key = qkv[pl.ds(r0, n), pl.ds(c0 + 256, PAD)]
            value = qkv[pl.ds(r0, n), pl.ds(c0 + 512, PAD)]
            scores = nt(query, key) * SCALE
            q_at = lax.broadcasted_iota(jnp.int32, (128, n), 0) + i * 128
            k_at = lax.broadcasted_iota(jnp.int32, (128, n), 1)
            scores = jnp.where(q_at >= k_at, scores, -1e30)
            expo = jnp.exp(scores - jnp.max(scores, axis=-1, keepdims=True))
            p = expo * (1.0 / jnp.sum(expo, axis=-1, keepdims=True))
            probs[u, i * 128 : (i + 1) * 128, :n] = p
            att[here, pl.ds(c0, PAD)] = nn(p.astype(LOW), value).astype(LOW)

    def one(at, body):
        loop(1, lambda i: body(at + i))

    def two(first, body):
        loop(2, lambda i: body(first + i))

    def out_parts(j):
        here = pl.ds(pl.multiple_of(j * 256, 256), 256)
        for i in range(10):
            cols = slice(i * 256, (i + 1) * 256)
            parts[here, cols] = nn(att[here, :], wo[:, cols]).astype(LOW)

    sources = (parts, backs)
    near = ((z + 4) % 8) // 2
    groups = (near, (near + 1) % 4, (near + 3) % 4, (near + 2) % 4)
    order = (4, 3, -3, 2, -2, 1, -1, 0)

    def core_copy(a, j):
        owner = (z + j + 8) % 8
        source = block(sources[a], owner, 1 - core)
        return remote(
            source, theirs.at[a, owner], core_send.at[a, j + 3], core_recv.at[a, j + 3], pair
        )

    def ring(a, way, k, q):
        sign = 1 if way == 0 else -1
        owner = (z + sign * (4 - k) + 8) % 8
        source = theirs.at[a, owner, chunks[q], :]
        if k == 0:
            target = first_buf.at[a, chunks[q], :]
        else:
            target = ring_buf.at[a, way, k - 1, chunks[q], :]
        device = up if way == 0 else down
        return remote(source, target, ring_send.at[a, way, k, q], ring_recv.at[a, way, k, q], device)

    def z_step(a, k, q):
        for way in range(2):
            if k < 4 - hops(way, q):
                continue
            j = (4 - k) * (1 if way == 0 else -1)
            owner = (z + j + 8) % 8
            own = block(sources[a], owner, core, q * half, half)
            other = theirs.at[a, owner, chunks[q], :]
            terms = [own, other]
            if k == 0:
                if q == 0:
                    core_copy(a, 4).wait_recv()
            else:
                if q == 0:
                    core_copy(a, j).wait_recv()
                if k > 4 - hops(way, q):
                    ring(a, way, k - 1, q).wait_recv()
                    if k == 1:
                        terms.append(first_buf.at[a, chunks[q], :])
                    else:
                        terms.append(ring_buf.at[a, way, k - 2, chunks[q], :])
            sum_into(other, terms)
            ring(a, way, k, q).start()

    send_list = [(way, k, q) for k in range(4) for q in range(2) for way in range(2) if k >= 4 - hops(way, q)]

    def swap_back(a, q):
        source, target = final.at[a, chunks[q], :], landed.at[a, chunks[q], :]
        return remote(source, target, back_send.at[a, q], back_recv.at[a, q], partner)

    def keep_back(a, q):
        source, target = final.at[a, chunks[q], :], landed.at[a, chunks[q], :]
        return pltpu.make_async_copy(source, target, back_local.at[a, q])

    def z_final(a, q):
        if q == 0:
            core_copy(a, 0).wait_recv()
        terms = [block(sources[a], z, core, q * half, half), theirs.at[a, z, chunks[q], :]]
        for way in range(2):
            ring(a, way, 3, q).wait_recv()
            terms.append(ring_buf.at[a, way, 2, chunks[q], :])
        sum_into(final.at[a, chunks[q], :], terms)

        @pl.when(place.away)
        def _():
            swap_back(a, q).start()

        @pl.when(place.home)
        def _():
            keep_back(a, q).start()

    def core_copies(a, js):
        for j in js:
            core_copy(a, j).start()

    one(0, project)
    advance(1, 0, 0)
    one(1, project)
    advance(1, 0, 1)
    one(2, project)
    advance(1, 1, 0)
    one(3, project)
    advance(1, 1, 1)
    one(0, forward)
    one(1, forward)
    advance(1, 2, 0)
    one(2, forward)
    one(3, forward)
    advance(1, 2, 1)
    one(groups[0], out_parts)
    core_copies(0, (4,))
    one(groups[1], out_parts)
    one(groups[2], out_parts)
    core_copies(0, (3, -3, 2, -2))
    z_step(0, 0, 0)
    z_step(0, 0, 1)
    one(groups[3], out_parts)
    core_copies(0, (1, -1, 0))
    def project_back(j):
        here = pl.ds(pl.multiple_of(j * 256, 256), 256)
        datt[here, :] = nt(c_full[here, :], wo[...]).astype(LOW)

    gathered(1, range(3))
    for group in (groups[3], groups[1], groups[2]):
        one(group, project_back)
    advance(1, 3, 0)
    advance(1, 3, 1)
    gathered(1, (3,))
    one(groups[0], project_back)

    def backward(u):
        r0, c0 = spots(u)
        for i in (3, 2, 1, 0):
            n = (i + 1) * 128
            here = pl.ds(r0 + i * 128, 128)
            query = qkv[here, pl.ds(c0, PAD)]
            key = qkv[pl.ds(r0, n), pl.ds(c0 + 256, PAD)]
            value = qkv[pl.ds(r0, n), pl.ds(c0 + 512, PAD)]
            d_att = datt[here, pl.ds(c0, PAD)]
            p = probs[u, i * 128 : (i + 1) * 128, :n]
            d_probs = nt(d_att, value)
            d_score = p * (d_probs - jnp.sum(d_probs * p, axis=-1, keepdims=True)) * SCALE
            d_low = d_score.astype(LOW)
            dqkv[here, pl.ds(c0, PAD)] = nn(d_low, key).astype(LOW)
            dk, dv = tn(d_low, query), tn(p.astype(LOW), d_att)
            if i == 3:
                dk_sum[...] = dk
                dv_sum[...] = dv
            else:
                dk_sum[:n, :] += dk
                dv_sum[:n, :] += dv
        dqkv[pl.ds(r0, LEN), pl.ds(c0 + 256, PAD)] = dk_sum[...].astype(LOW)
        dqkv[pl.ds(r0, LEN), pl.ds(c0 + 512, PAD)] = dv_sum[...].astype(LOW)

    z_step(0, 1, 0)
    one(0, backward)
    z_step(0, 1, 1)
    two(1, backward)
    z_step(0, 2, 0)
    one(3, backward)

    def turn(i):
        for j in range(4):
            cut = slice(j * 256, (j + 1) * 256)
            source = dqkv[cut, i * 256 : (i + 1) * 256] if i < 3 else att[cut, :]
            backs[i * 256 : (i + 1) * 256, cut] = source.T

    def weight_grads(s, q):
        for i in (2 * s, 2 * s + 1):
            factor = backs[i * 256 : (i + 1) * 256, 0:1024]
            total = nn(factor, (x_full if i < 3 else c_full)[:, columns(q)]).astype(LOW)
            for h in range(2):
                spot = i * 160 + h * HEAD_DIM
                g[spot : spot + HEAD_DIM, columns(q)] = total[h * PAD : h * PAD + HEAD_DIM, :]

    side_start, side_rows, subs, width = (0, 320), (320, 320), (80, 80), dim // 4
    firsts, seconds = (x, y), (y, x)
    neighbours = ((right, left), (north, south))
    lanes = (slice(0, 384), slice(384, 640))
    pieces = [(s, c) for c in range(2) for s in range(2)]

    def half_of(s, way, size):
        count = (size[s] // 16 + 1) // 2 * 16
        return slice(0, count) if way == 0 else slice(count, size[s])

    def columns(q):
        return pl.ds(pl.multiple_of(((q + 4) % 4) * width, 128), width)

    def g_side(s, q, c):
        return g.at[pl.ds(side_start[s], side_rows[s]), columns(q)].at[:, lanes[c]]

    def sub_rows(s, q):
        return pl.ds(pl.multiple_of(((q + 4) % 4) * subs[s], 16), subs[s])

    def e_sub(s, q, c):
        return e_sum.at[s, sub_rows(s, q), lanes[c]]

    def step_to(s, way, places):
        return places[s] + (1 if way == 0 else -1)

    def f_copy(s, way, k, c):
        device = neighbours[s][way]
        sems = (f_send.at[s, way, k, c], f_recv.at[s, way, k, c])
        if k == 0:
            part = half_of(s, way, side_rows)
            source = g_side(s, firsts[s] + 2, c).at[part, :]
            return remote(source, f_first.at[s, part, lanes[c]], *sems, device)
        source = g_side(s, step_to(s, way, firsts), c)
        return remote(source, f_buf.at[s, way, 0 : side_rows[s], lanes[c]], *sems, device)

    def s_copy(s, way, k, c):
        device = neighbours[1 - s][way]
        sems = (s_send.at[s, way, k, c], s_recv.at[s, way, k, c])
        if k == 0:
            part = half_of(s, way, subs)
            source = e_sub(s, seconds[s] + 2, c).at[part, :]
            return remote(source, s_first.at[s, part, lanes[c]], *sems, device)
        source = e_sub(s, step_to(s, way, seconds), c)
        return remote(source, s_buf.at[s, way, 0 : subs[s], lanes[c]], *sems, device)

    def f_pass(s, c):
        for way in range(2):
            f_copy(s, way, 0, c).wait_recv()
            part = half_of(s, way, side_rows)
            own = g_side(s, step_to(s, way, firsts), c).at[part, :]
            sum_into(own, [own, f_first.at[s, part, lanes[c]]])
            f_copy(s, way, 1, c).start()

    def f_final(s, c):
        for way in range(2):
            f_copy(s, way, 1, c).wait_recv()
        came = [f_buf.at[s, way, 0 : side_rows[s], lanes[c]] for way in range(2)]
        sum_into(e_sum.at[s, 0 : side_rows[s], lanes[c]], [g_side(s, firsts[s], c)] + came)
        for way in range(2):
            s_copy(s, way, 0, c).start()

    def s_pass(s, c):
        for way in range(2):
            s_copy(s, way, 0, c).wait_recv()
            part = half_of(s, way, subs)
            own = e_sub(s, step_to(s, way, seconds), c).at[part, :]
            sum_into(own, [own, s_first.at[s, part, lanes[c]]])
            s_copy(s, way, 1, c).start()

    def work(s, row, col, c):
        start = pl.multiple_of(side_start[s] + ((row + 4) % 4) * subs[s], 16)
        return g_work.at[pl.ds(start, subs[s]), columns(col)].at[:, lanes[c]]

    def work_column(s, col, c):
        return g_work.at[pl.ds(side_start[s], side_rows[s]), columns(col)].at[:, lanes[c]]

    def s_final(s, c):
        for way in range(2):
            s_copy(s, way, 1, c).wait_recv()
        came = [s_buf.at[s, way, 0 : subs[s], lanes[c]] for way in range(2)]
        sum_into(work(s, seconds[s], firsts[s], c), [e_sub(s, seconds[s], c)] + came)

    def ya(s, way, k, c):
        device = north if way == 0 else south
        at = y if k == 0 else (y - 1 if way == 0 else y + 1)
        if s == 0:
            spot, size = work(0, at, x, c), subs
        else:
            spot, size = work_column(1, at, c), side_rows
        if k == 1:
            spot = spot.at[half_of(s, way, size), :]
        return remote(spot, spot, ga_send.at[s, way, k, c], ga_recv.at[s, way, k, c], device)

    def xa(s, i, c):
        spot = work_column(0, x, c) if s == 0 else work(1, x, y, c)
        device = (right, left, across)[i]
        return remote(spot, spot, gh_send.at[s, i, c], gh_recv.at[s, i, c], device)

    def xa_came(s, i, c):
        source = (x - 1, x + 1, x + 2)[i]
        spot = work_column(0, source, c) if s == 0 else work(1, source, y, c)
        return remote(spot, spot, gh_send.at[s, i, c], gh_recv.at[s, i, c], pair)

    relay_in = remote(
        work_column(0, x, 1), work_column(0, x, 1), relay_send, relay_recv, left
    )
    relay_out = remote(
        work_column(0, x + 1, 1),
        work_column(0, x + 1, 1),
        gh_send.at[0, 2, 1],
        gh_recv.at[0, 2, 1],
        left,
    )

    def xa_start(s, c):
        @pl.when(place.away)
        def _():
            xa(s, 0, c).start()
            xa(s, 1, c).start()

        @pl.when(place.home)
        def _():
            if (s, c) == (0, 1):
                relay_in.start()
            else:
                xa(s, 2, c).start()

    def handed(s, i, c):
        at = x if s == 0 else y
        place_of = columns((at, at - 1, at + 1, at + 2)[i])
        return lambda ref: ref.at[pl.ds(side_start[s], side_rows[s]), place_of].at[:, lanes[c]]

    def hand_pair(s, i, c):
        spot = handed(s, i, c)
        return remote(spot(g_work), spot(g_out), go_send.at[s, i, c], go_recv.at[s, i, c], pair)

    def hand_out(s, i, c):
        spot = handed(s, i, c)
        return pltpu.make_async_copy(spot(g_work), spot(g_out), go_local.at[s, i, c])

    def hand(s, i, c):
        hand_pair(s, i, c).start()
        hand_out(s, i, c).start()

    def y_start(c):
        for way in range(2):
            ya(0, way, 0, c).start()
        xa_start(1, c)

    def y_pass(c):
        for way in range(2):
            ya(0, way, 0, c).wait_recv()
            ya(0, way, 1, c).start()

    def y_final(c):
        for way in range(2):
            ya(0, way, 1, c).wait_recv()
        xa_start(0, c)

    def f_start(s):
        for c in range(2):
            for way in range(2):
                f_copy(s, way, 0, c).start()

    turn(0)
    turn(1)
    weight_grads(0, x + 2)
    f_start(0)
    z_step(0, 2, 1)
    turn(2)
    turn(3)
    weight_grads(1, y + 2)
    f_start(1)
    weight_grads(0, x + 1)
    weight_grads(0, x - 1)
    f_pass(0, 0)
    f_pass(0, 1)
    z_step(0, 3, 0)
    weight_grads(1, y + 1)
    weight_grads(1, y - 1)
    f_pass(1, 0)
    f_pass(1, 1)
    z_step(0, 3, 1)
    weight_grads(0, x)
    weight_grads(1, y)

    def back_parts(j):
        here = pl.ds(pl.multiple_of(j * 256, 256), 256)
        for i in range(10):
            cols = slice(i * 256, (i + 1) * 256)
            backs[here, cols] = nn(dqkv[here, :], wq[:, cols]).astype(LOW)

    one(groups[0], back_parts)
    core_copies(1, (4,))
    one(groups[1], back_parts)
    z_step(1, 0, 0)
    z_step(1, 0, 1)
    one(groups[2], back_parts)
    core_copies(1, (3, -3, 2, -2))
    f_final(0, 0)
    z_final(0, 0)
    z_step(1, 1, 0)
    one(groups[3], back_parts)
    core_copies(1, (1, -1, 0))
    z_final(0, 1)
    z_step(1, 1, 1)
    f_final(1, 0)
    z_step(1, 2, 0)
    s_pass(0, 0)
    s_pass(1, 0)
    f_final(0, 1)
    f_final(1, 1)
    z_step(1, 2, 1)
    s_pass(0, 1)
    s_pass(1, 1)
    s_final(0, 0)
    s_final(1, 0)
    y_start(0)
    z_step(1, 3, 0)
    s_final(0, 1)
    s_final(1, 1)
    y_start(1)
    y_pass(0)
    z_step(1, 3, 1)
    y_pass(1)
    y_final(0)

    @pl.when(place.home)
    def _():
        for c in range(2):
            for i in range(3):
                xa_came(1, i, c).wait_recv()
            for way in range(2):
                ya(1, way, 0, c).start()
            hand(1, 0, c)
            if c == 0:
                hand(0, 0, 0)

    y_final(1)

    @pl.when(place.home)
    def _():
        hand(0, 0, 1)
        for c in range(2):
            for way in range(2):
                ya(1, way, 0, c).wait_recv()
                ya(1, way, 1, c).start()
                hand(1, 1 + way, c)

    def landing(a):
        @pl.when(place.away)
        def _():
            for q in range(2):
                swap_back(a, q).wait_recv()

        @pl.when(place.home)
        def _():
            for q in range(2):
                keep_back(a, q).wait()

    def finish_output(i):
        here = pl.ds(pl.multiple_of(i * 16, 16), 16)
        out_ref[here, :] = (tokens[here, :].astype(WIDE) + landed[0, here, :].astype(WIDE)).astype(LOW)

    def finish_gradient(i):
        here = pl.ds(pl.multiple_of(i * 32, 32), 32)
        xhat, rstd = standardize(tokens[here, :])
        scaled = landed[1, here, :].astype(WIDE) * gain[...].reshape(1, dim)
        first = jnp.mean(scaled, axis=-1, keepdims=True)
        second = jnp.mean(scaled * xhat, axis=-1, keepdims=True)
        total = cot[here, :].astype(WIDE) + rstd * (scaled - first - xhat * second)
        ingrad_ref[here, :] = total.astype(LOW)

    landing(0)
    loop(rows // 16, finish_output)
    z_final(1, 0)
    z_final(1, 1)
    @pl.when(place.away)
    def _():
        relay_in.wait_recv()
        relay_out.start()

    landing(1)
    loop(rows // 32, finish_gradient)

    @pl.when(place.home)
    def _():
        for c in range(2):
            for way in range(2):
                ya(1, way, 1, c).wait_recv()
            hand(1, 3, c)
        for c in range(2):
            for i in range(3):
                xa_came(0, i, c).wait_recv()
                hand(0, 1 + i, c)

    @pl.when(place.away)
    def _():
        for s, c in pieces:
            for i in range(4):
                hand_pair(s, i, c).wait_recv()
            xa(s, 0, c).wait_send()
            xa(s, 1, c).wait_send()
        relay_out.wait_send()
        for a, q in both:
            swap(a, q).wait_send()
            swap_back(a, q).wait_send()
        for i, h in weights:
            weight_swap(i, h).wait_send()

    @pl.when(place.home)
    def _():
        for s, c in pieces:
            for i in range(4):
                hand_pair(s, i, c).wait_send()
                hand_out(s, i, c).wait()
            if (s, c) == (0, 1):
                relay_in.wait_send()
            else:
                xa(s, 2, c).wait_send()
        for way, k in both:
            for c in range(2):
                ya(1, way, k, c).wait_send()

    for a in range(2):
        for q in range(2):
            own_pair(a, q).wait_send()
        for way, k, q in hop_list:
            gather(a, way, k, q).wait_send()
            to_pair(a, way, k, q).wait_send()
        for j in order:
            core_copy(a, j).wait_send()
        for way, k, q in send_list:
            ring(a, way, k, q).wait_send()
    for way, k in both:
        for c in range(2):
            ya(0, way, k, c).wait_send()
            for s in range(2):
                f_copy(s, way, k, c).wait_send()
                s_copy(s, way, k, c).wait_send()


def run_layer(tokens, gain, w_qkv, w_out, cotangent):
    rows, dim = tokens.shape
    vmem = pl.BlockSpec(memory_space=pltpu.VMEM)
    any_space = pl.BlockSpec(memory_space=pl.ANY)
    dma = pltpu.SemaphoreType.DMA
    sums = 4 * w_out.shape[0]
    quarter = dim // 4

    def low(*shape):
        return pltpu.VMEM(shape, LOW)

    return pl.pallas_call(
        layer_kernel,
        out_shape=(
            jax.ShapeDtypeStruct((rows, dim), LOW),
            jax.ShapeDtypeStruct((rows, dim), LOW),
            jax.ShapeDtypeStruct((sums, dim), LOW),
        ),
        in_specs=[vmem, vmem, any_space, any_space, vmem],
        out_specs=(vmem, vmem, any_space),
        scratch_shapes=[
            low(rows, dim),
            low(rows * 16, dim),
            low(rows * 16, dim),
            low(6 * PAD, dim),
            low(2 * PAD, dim),
            low(rows * 16, 6 * PAD),
            low(rows * 16, 2 * PAD),
            low(rows * 16, 2 * PAD),
            low(rows * 16, 6 * PAD),
            pltpu.VMEM((4, LEN, LEN), WIDE),
            pltpu.VMEM((LEN, PAD), WIDE),
            pltpu.VMEM((LEN, PAD), WIDE),
            low(rows * 16, dim),
            low(rows * 16, dim),
            low(2, 8, rows, dim),
            low(2, rows, dim),
            low(2, 2, 3, rows, dim),
            low(2, rows, dim),
            low(2, rows, dim),
            low(sums, dim),
            low(2, 320, quarter),
            low(2, 2, 320, quarter),
            low(2, 320, quarter),
            low(2, 80, quarter),
            low(2, 2, 80, quarter),
            low(sums, dim),
            dma((2, 2)),
            dma((2, 2)),
            dma((2, 2)),
            dma((4, 2)),
            dma((4, 2)),
            dma((4, 2)),
            dma((2, 2, 4, 2)),
            dma((2, 2, 4, 2)),
            dma((2, 2)),
            dma((2, 2)),
            dma((2, 2, 4, 2)),
            dma((2, 2, 4, 2)),
            dma((2, 8)),
            dma((2, 8)),
            dma((2, 2, 4, 2)),
            dma((2, 2, 4, 2)),
            dma((2, 2)),
            dma((2, 2)),
            dma((2, 2)),
            dma((2, 2, 2, 2)),
            dma((2, 2, 2, 2)),
            dma((2, 2, 2, 2)),
            dma((2, 2, 2, 2)),
            dma((2, 2, 2, 2)),
            dma((2, 2, 2, 2)),
            dma((2, 3, 2)),
            dma((2, 3, 2)),
            dma((2, 4, 2)),
            dma((2, 4, 2)),
            dma((2, 4, 2)),
            dma,
            dma,
        ],
        compiler_params=pltpu.CompilerParams(
            collective_id=0, has_side_effects=True, vmem_limit_bytes=VMEM_BYTES
        ),
        name="attention_layer",
    )(tokens, gain, w_qkv, w_out, cotangent)


def widen_kernel(sums, out_in, ingrad_in, gq, go, out, ingrad, low_buf, wide_buf, in_sem, out_sem):
    count, split = 80, gq.shape[0]
    scale = 1.0 / lax.axis_size("dp")

    def fetch(i):
        spot = slice(i * count, (i + 1) * count)
        return pltpu.make_async_copy(sums.at[spot, :], low_buf.at[spot, :], in_sem.at[i])

    def store(i):
        first = i * count
        source = wide_buf.at[first : first + count, :]
        ref, at = (gq, first) if first < split else (go, first - split)
        return pltpu.make_async_copy(source, ref.at[at : at + count, :], out_sem.at[i])

    steps = sums.shape[0] // count
    for i in range(steps):
        fetch(i).start()
    out[...] = out_in[...]
    ingrad[...] = ingrad_in[...]
    for i in range(steps):
        fetch(i).wait()

        def widen(k):
            here = pl.ds(pl.multiple_of(i * count + k * 16, 16), 16)
            wide_buf[here, :] = low_buf[here, :].astype(WIDE) * scale

        loop(count // 16, widen)
        store(i).start()
    for i in range(steps):
        store(i).wait()


def widen_sums(sums, output, input_gradient, width):
    total, dim = sums.shape
    vmem = pl.BlockSpec(memory_space=pltpu.VMEM)
    any_space = pl.BlockSpec(memory_space=pl.ANY)
    return pl.pallas_call(
        widen_kernel,
        out_shape=(
            jax.ShapeDtypeStruct((3 * width, dim), WIDE),
            jax.ShapeDtypeStruct((total - 3 * width, dim), WIDE),
            jax.ShapeDtypeStruct(output.shape, LOW),
            jax.ShapeDtypeStruct(output.shape, LOW),
        ),
        in_specs=[any_space, vmem, vmem],
        out_specs=(any_space, any_space, vmem, vmem),
        scratch_shapes=[
            pltpu.VMEM((total, dim), LOW),
            pltpu.VMEM((total, dim), WIDE),
            pltpu.SemaphoreType.DMA((8,)),
            pltpu.SemaphoreType.DMA((8,)),
        ],
        compiler_params=pltpu.CompilerParams(vmem_limit_bytes=VMEM_BYTES),
        name="widen_sums",
    )(sums, output, input_gradient)


def per_device(tokens, gain, w_qkv, w_out, cotangent):
    width = w_out.shape[0]
    output, input_gradient, sums = run_layer(tokens, gain, w_qkv, w_out, cotangent)
    grad_qkv, grad_out, output, input_gradient = widen_sums(sums, output, input_gradient, width)
    return (output, input_gradient, grad_qkv.reshape(w_qkv.shape), grad_out)


def solution(mesh):
    placed = (
        P(("dp", "tensor"), None),
        P(),
        P(None, "tensor", None),
        P("tensor", None),
        P(("dp", "tensor"), None),
    )
    return jax.shard_map(
        per_device,
        mesh=mesh,
        in_specs=placed,
        out_specs=(
            P(("dp", "tensor"), None),
            P(("dp", "tensor"), None),
            P(None, "tensor", None),
            P("tensor", None),
        ),
        check_vma=False,
    )
```
